256 devices in a mesh: dev: 256 (over z, y, x, core).
Axes of the slice: x: 4, y: 4, z: 8, core: 2. Of those that a mesh axis runs over, the one named last changes fastest.
Arguments:
- vectors: bfloat16 [8, 4194304], P(None, 'dev'), may hold values from -1.5 to 1.5
- points: float32 [3, 4194304], P(None, 'dev'), may hold values from -4 to 4
- leaf_basis: bfloat16 [16384, 64, 256], P('dev'), may hold values from -0.375 to 0.375
- near_list: int32 [16384, 8], P('dev'), may hold values from -32 to 32, as said below
- far_list: int32 [15872, 4], P('dev'), may hold values from -32 to 32, as said below
- transfer: bfloat16 [16128, 64, 128], P('dev'), may hold values from -0.625 to 0.625
- skeleton: float32 [16128, 192], P('dev'), may hold values from -4 to 4
- transfer_top: bfloat16 [255, 64, 128], replicated, may hold values from -0.625 to 0.625
- skeleton_top: float32 [254, 192], replicated, may hold values from -4 to 4
Outputs:
- product: float32 [8, 4194304], P(None, 'dev')
The draws below stay inside these ranges and needn't reach their ends.
Inputs may be any that keep to these rules, and one draw needn't show every extreme that they name: `near_list`: slot 0 of every row holds 0 (the leaf itself); every other slot holds 0 (empty) or a nonzero offset such that the leaf plus the offset is a leaf; the nonzero offsets of a row are distinct. `far_list`: rows follow the numbering of the transfer rows of levels 1 to log2(64) - 1. An entry is 0 (empty) or a nonzero offset of magnitude 2 or more and at most that level's clusters on one device, such that the cluster plus the offset is a cluster of the same level; the nonzero offsets of a row are distinct.
All inputs are finite; a program needn't handle non-finite values.
Results may differ from the reference program's by a relative error of at most 0.002.
Values may be sent and summed in bfloat16 or wider, within the bound.
No kernel may reach another device: no remote copies, remote signals or barrier semaphores. Data moves between devices by JAX's collectives and lax.ppermute only.
A program may use at most 64 MiB of HBM per device.

```python
import jax
import jax.numpy as jnp
import numpy as np
from jax import lax

LEAF = 256
RANK = 64
RHS = 8
LEAF_DEV = 64
NEAR_SLOTS = 8
FAR_SLOTS = 4
LEAVES = 16384
POINTS = 4194304
PARENTS = 16128
TOP_ROWS = 255
TOP_SKELETONS = 254
N_DEV = 256


def choose_offsets(key, candidates, allowed, wanted, width):
    column_count = candidates.shape[1]
    ranking = jax.random.randint(key, candidates.shape, 0, 1 << 20)
    column = jnp.arange(column_count, dtype=jnp.int32)[None, :]
    scores = jnp.where(allowed, ranking * column_count + column, -1 - column)
    taken_count = min(width, column_count)
    best_scores, best_index = lax.top_k(scores, taken_count)
    picked = jnp.take_along_axis(candidates, best_index, axis=1)
    keeping = (best_scores >= 0) & (jnp.arange(taken_count, dtype=jnp.int32)[None, :] < wanted[:, None])
    picked = jnp.where(keeping, picked, 0).astype(jnp.int32)
    if taken_count < width:
        picked = jnp.concatenate([picked, jnp.zeros((picked.shape[0], width - taken_count), jnp.int32)], axis=1)
    return picked


def draw_near_list(key, part):
    key = jax.random.fold_in(key, 11)
    leaf_total = LEAF_DEV * N_DEV
    reach_leaves = LEAF_DEV // 2
    column = np.arange(2 * reach_leaves)
    magnitude = column // 2 + 1
    offsets_row = np.where(column % 2 == 0, magnitude, -magnitude).astype(np.int32)
    leaf_ids = np.arange(leaf_total, dtype=np.int32)[:, None]
    candidates = np.broadcast_to(offsets_row[None, :], (leaf_total, 2 * reach_leaves)).astype(np.int32)
    allowed = (leaf_ids + candidates >= 0) & (leaf_ids + candidates < leaf_total)
    key_dense, key_count, key_pick = jax.random.split(key, 3)
    dense_device = jax.random.randint(key_dense, (N_DEV,), 0, 4) == 0
    ceiling = jnp.repeat(jnp.where(dense_device, NEAR_SLOTS - 1, 1), LEAF_DEV)
    wanted = jax.random.randint(key_count, (leaf_total,), 0, 1 << 20) % ceiling + 1
    extra_slots = choose_offsets(key_pick, jnp.asarray(candidates), jnp.asarray(allowed), wanted, NEAR_SLOTS - 1)
    return jnp.concatenate([jnp.zeros((leaf_total, 1), jnp.int32), extra_slots], axis=1)


def draw_far_list(key, part):
    key = jax.random.fold_in(key, 23)
    level_counts = []
    local_index = []
    for level_index in range(1, LEAF_DEV.bit_length() - 1):
        level_count = LEAF_DEV >> level_index
        level_counts.extend([level_count] * level_count)
        local_index.extend(range(level_count))
    level_counts = np.tile(np.asarray(level_counts, np.int64), N_DEV)
    local_index = np.tile(np.asarray(local_index, np.int64), N_DEV)
    device_ids = np.repeat(np.arange(N_DEV, dtype=np.int64), LEAF_DEV - 2)
    global_index = device_ids * level_counts + local_index
    column_count = LEAF_DEV - 2
    column = np.arange(column_count)
    magnitude = column // 2 + 2
    offsets_row = np.where(column % 2 == 0, magnitude, -magnitude)
    candidates = np.broadcast_to(offsets_row[None, :], (level_counts.shape[0], column_count))
    target = global_index[:, None] + candidates
    allowed = (magnitude[None, :] <= level_counts[:, None]) & (target >= 0) & (target < (level_counts * N_DEV)[:, None])
    key_count, key_pick = jax.random.split(key, 2)
    wanted = jax.random.randint(key_count, (level_counts.shape[0],), 1, FAR_SLOTS + 1)
    return choose_offsets(key_pick, jnp.asarray(candidates.astype(np.int32)), jnp.asarray(allowed), wanted, FAR_SLOTS)


def levels(key, dims, pieces, low, high):
    gain, own = 1.0, jax.random.fold_in(key, 6)
    for position, shards_of in pieces:
        steps = jnp.exp(jax.random.uniform(jax.random.fold_in(own, position), (shards_of,), jnp.float32, low / len(pieces), high / len(pieces)))
        gain = gain * jnp.repeat(steps, dims[position] // shards_of).reshape([-1 if axis == position else 1 for axis in range(len(dims))])
    return gain


def bell_draw(own_key, extent, scale, reach, shards=(), held_as=jnp.bfloat16):
    array = jax.random.normal(own_key, extent, jnp.float32) * scale
    if len(shards) > 0:
        array = levels(own_key, extent, shards, -0.22, 0.18) * array
    return jnp.clip(array, min=-reach, max=reach).astype(held_as)


def setup_inputs(seed: int = 0) -> dict:
    seeds = jax.random.split(jax.random.key(seed), 10)
    vectors = bell_draw(seeds[0], (RHS, POINTS), 0.25, 1.5, ((1, 256),))
    points = bell_draw(seeds[1], (3, POINTS), 1.0, 4.0, ((1, 256),), jnp.float32)
    leaf_basis = bell_draw(seeds[2], (LEAVES, RANK, LEAF), LEAF ** -0.5, 0.375, ((0, 256),))
    near_list = draw_near_list(jax.random.fold_in(seeds[9], 71), 0)
    far_list = draw_far_list(jax.random.fold_in(seeds[9], 71), 0)
    transfer = bell_draw(seeds[5], (PARENTS, RANK, 2 * RANK), (7 * RANK // 5) ** -0.5, 0.625, ((0, 256),))
    skeleton = bell_draw(seeds[6], (PARENTS, 3 * RANK), 1.0, 4.0, ((0, 256),), jnp.float32)
    transfer_top = bell_draw(seeds[7], (TOP_ROWS, RANK, 2 * RANK), (7 * RANK // 5) ** -0.5, 0.625)
    skeleton_top = bell_draw(seeds[8], (TOP_SKELETONS, 3 * RANK), 1.0, 4.0, (), jnp.float32)
    return {"vectors": vectors, "points": points, "leaf_basis": leaf_basis, "near_list": near_list, "far_list": far_list, "transfer": transfer, "skeleton": skeleton, "transfer_top": transfer_top, "skeleton_top": skeleton_top}


highest = lax.Precision.HIGHEST

def kernel_block(targets, sources):
    spacing = targets[..., 0, :, None] - sources[..., 0, None, :]
    squares = spacing * spacing
    for component in (1, 2):
        spacing = targets[..., component, :, None] - sources[..., component, None, :]
        squares = squares + spacing * spacing
    return jnp.exp(-jnp.sqrt(squares))

def join_children(children):
    pair_count = children.shape[0] // 2
    joined = children.reshape(pair_count, 2, children.shape[1], children.shape[2]).transpose(0, 2, 1, 3)
    return joined.reshape(pair_count, children.shape[1], 2 * children.shape[2])

def split_children(joined, rank_size):
    parent_count = joined.shape[0]
    halves = joined.reshape(parent_count, joined.shape[1], 2, rank_size).transpose(0, 2, 1, 3)
    return halves.reshape(2 * parent_count, joined.shape[1], rank_size)

def lift_level(children, matrices):
    return jnp.einsum('mkj,mrj->mkr', children.astype(jnp.float32), matrices.astype(jnp.float32), precision=highest)

def lower_level(parents, matrices):
    return jnp.einsum('mkr,mrj->mkj', parents, matrices.astype(jnp.float32), precision=highest)

def swap_pairs(values):
    pair_count = values.shape[0] // 2
    return values.reshape((pair_count, 2) + values.shape[1:])[:, ::-1].reshape(values.shape)

def couple_sibling(skeletons, coefficients):
    tile_block = kernel_block(skeletons, swap_pairs(skeletons))
    return jnp.einsum('mij,mkj->mki', tile_block, swap_pairs(coefficients), precision=highest)

def reference(vectors, points, leaf_basis, near_list, far_list, transfer, skeleton, transfer_top, skeleton_top):
    local_levels = LEAF_DEV.bit_length() - 1
    top_levels = N_DEV.bit_length() - 1
    leaf_total = LEAF_DEV * N_DEV
    leaf_vectors = vectors.reshape(RHS, leaf_total, LEAF)
    leaf_points = points.reshape(3, leaf_total, LEAF).transpose(1, 0, 2)

    def near_block(block_index):
        first_leaf = block_index * LEAF_DEV
        targets = first_leaf + jnp.arange(LEAF_DEV, dtype=jnp.int32)
        offsets = lax.dynamic_slice_in_dim(near_list, first_leaf, LEAF_DEV, 0)
        usable = (jnp.arange(NEAR_SLOTS, dtype=jnp.int32)[None, :] == 0) | (offsets != 0)
        partners = jnp.clip(targets[:, None] + offsets, 0, leaf_total - 1).astype(jnp.int32)
        own_points = lax.dynamic_slice_in_dim(leaf_points, first_leaf, LEAF_DEV, 0)[:, None]
        tile_block = kernel_block(own_points, leaf_points[partners])
        tile_block = jnp.where(usable[:, :, None, None], tile_block, 0.0).astype(jnp.bfloat16)
        tile_block = lax.optimization_barrier(tile_block).astype(jnp.float32)
        sources = leaf_vectors[:, partners].astype(jnp.float32)
        return jnp.einsum('bsij,kbsj->kbi', tile_block, sources, precision=highest)
    near_blocks = lax.map(near_block, jnp.arange(N_DEV, dtype=jnp.int32))
    near_part = near_blocks.transpose(1, 0, 2, 3).reshape(RHS, leaf_total, LEAF)
    coefficients = [jnp.einsum('kti,tri->tkr', leaf_vectors.astype(jnp.float32), leaf_basis.astype(jnp.float32), precision=highest)]
    local_transfer = transfer.reshape(N_DEV, LEAF_DEV - 1, RANK, 2 * RANK)
    local_skeleton = skeleton.reshape(N_DEV, LEAF_DEV - 1, 3, RANK)
    local_far = far_list.reshape(N_DEV, LEAF_DEV - 2, FAR_SLOTS)
    transfers = [None]
    skeletons = [None]
    far_lists = [None]
    for level_index in range(1, local_levels + 1):
        first_row = LEAF_DEV - (LEAF_DEV >> level_index - 1)
        level_count = LEAF_DEV >> level_index
        transfers.append(local_transfer[:, first_row:first_row + level_count].reshape(-1, RANK, 2 * RANK))
        skeletons.append(local_skeleton[:, first_row:first_row + level_count].reshape(-1, 3, RANK))
        if level_index < local_levels:
            far_lists.append(local_far[:, first_row:first_row + level_count].reshape(-1, FAR_SLOTS))
    for step_index in range(1, top_levels + 1):
        first_row = N_DEV - (N_DEV >> step_index - 1)
        level_count = N_DEV >> step_index
        transfers.append(transfer_top[first_row:first_row + level_count])
        if step_index < top_levels:
            skeletons.append(skeleton_top[first_row:first_row + level_count].reshape(level_count, 3, RANK))
    all_levels = local_levels + top_levels
    for level_index in range(1, all_levels):
        coefficients.append(lift_level(join_children(coefficients[-1]), transfers[level_index]))
    downward = jnp.zeros((1, RHS, RANK), jnp.float32)
    for level_index in range(all_levels - 1, -1, -1):
        downward = split_children(lower_level(downward, transfers[level_index + 1]), RANK)
        if level_index >= local_levels:
            downward = downward + couple_sibling(skeletons[level_index], coefficients[level_index])
        elif level_index >= 1:
            level_count = coefficients[level_index].shape[0]
            for slot_index in range(FAR_SLOTS):
                offsets = far_lists[level_index][:, slot_index]
                partners = jnp.clip(jnp.arange(level_count, dtype=jnp.int32) + offsets, 0, level_count - 1).astype(jnp.int32)
                tile_block = kernel_block(skeletons[level_index], skeletons[level_index][partners])
                tile_block = jnp.where((offsets != 0)[:, None, None], tile_block, 0.0)
                downward = downward + jnp.einsum('mij,mkj->mki', tile_block, coefficients[level_index][partners], precision=highest)
    far_part = jnp.einsum('tkr,tri->kti', downward, leaf_basis.astype(jnp.float32), precision=highest)
    return (near_part + far_part).reshape(RHS, leaf_total * LEAF)
```

```python
import functools

import jax
import jax.numpy as jnp
from jax import lax
from jax.experimental import pallas as pl
from jax.experimental.pallas import tpu as pltpu
from jax.sharding import PartitionSpec as P

f32 = jnp.float32
bf16 = jnp.bfloat16
LEAVES = 64
POINTS = 256
REACH = 32
RANK = 64
UNROLL = 16
PIECES = 4
LIST = 512 + UNROLL
VM = pl.BlockSpec(memory_space=pltpu.VMEM)
SM = pl.BlockSpec(memory_space=pltpu.SMEM)
HB = pl.BlockSpec(memory_space=pl.ANY)


def params(mib):
    return pltpu.CompilerParams(vmem_limit_bytes=mib << 20)


def nt(a, b):
    return lax.dot_general(a, b, (((1,), (1,)), ((), ())), preferred_element_type=f32)


def nn(a, b):
    return jnp.dot(a, b, preferred_element_type=f32)


def split(x):
    high = x.astype(bf16)
    low = (x - high.astype(f32)).astype(bf16)
    return high, low


def low_lanes(shape):
    return lax.broadcasted_iota(jnp.int32, shape, 1) < RANK


def kernel_value(squares):
    return jnp.exp(-(squares * lax.rsqrt(jnp.maximum(squares, 1e-30))))


def prep_kernel(points, vectors, left, right):
    step = 2048
    row = lax.broadcasted_iota(jnp.int32, (8, step), 0)
    for start in range(0, 16384, step):
        p = points[:, start : start + step]
        p = jnp.concatenate([p, jnp.zeros((5, step), f32)], axis=0)
        a1 = jnp.round(p * 64.0) * (1.0 / 64.0)
        rest = p - a1
        a2 = jnp.round(rest * 16384.0) * (1.0 / 16384.0)
        a3 = (rest - a2).astype(bf16).astype(f32)
        rest = a2 + a3
        big = jnp.sum(a1 * a1, axis=0, keepdims=True)
        small = jnp.sum((2.0 * a1 + rest) * rest, axis=0, keepdims=True)
        n1 = jnp.floor(big * 4.0) * 0.25
        big = big - n1
        n2 = jnp.floor(big * 1024.0) * (1.0 / 1024.0)
        value = (big - n2) + small
        n3 = value.astype(bf16).astype(f32)
        value = value - n3
        n4 = value.astype(bf16).astype(f32)
        n5 = value - n4
        upper = a1 + pltpu.roll(a2, 4, 0)
        upper = jnp.where((row == 3) | (row == 7), 1.0, upper)
        lower = jnp.where(row == 3, n1, a3)
        lower = jnp.where(row == 4, n2, lower)
        lower = jnp.where(row == 5, n3, lower)
        lower = jnp.where(row == 6, n4, lower)
        lower = jnp.where(row == 7, n5, lower)
        v = vectors[:, start : start + step].astype(f32)
        packed = jnp.concatenate([upper, lower, v, jnp.zeros_like(v)], axis=0).astype(bf16)
        half, at = (left, start) if start < 8192 else (right, start - 8192)
        half[:, at : at + step] = packed


def prep(points, vectors):
    shape = jax.ShapeDtypeStruct((32, 8192), bf16)
    return pl.pallas_call(
        prep_kernel,
        out_shape=(shape, shape),
        in_specs=[VM, VM],
        out_specs=(VM, VM),
        compiler_params=params(24),
        name="prep",
    )(points, vectors)


def selection():
    import numpy as np

    table = np.zeros((16, 48), np.float32)
    for copy, base in enumerate((0, 4, 8)):
        for block in (0, 4, 8):
            for c in range(3):
                table[base + c, copy * 16 + block + c] = -2.0
    for r in range(11, 16):
        table[3, r] = 1.0
    for n, col in enumerate((3, 7, 19, 23, 35)):
        table[11 + n, col] = 1.0
    return table


def up_kernel(
    left, right, vectors, leaf_basis, near_list, transfer, skeleton, select, table, root, targets, tiles, count
):
    def leaf_list(t, at):
        for s in range(8):
            offset = near_list[t, s]
            tiles[at] = t * 128 + t + REACH + offset
            if s == 0:
                at = at + 1
            else:
                at = at + jnp.where(offset != 0, 1, 0)
        return at

    total = lax.fori_loop(0, LEAVES, leaf_list, jnp.int32(0), unroll=4)
    for s in range(UNROLL):
        tiles[total + s] = LEAVES * 128 + REACH
    count[0] = total

    low = low_lanes((8, 128))
    joined = []
    for c in range(LEAVES // 2):
        a = vectors[:, c * 512 : c * 512 + 256].astype(f32)
        b = vectors[:, c * 512 + 256 : c * 512 + 512].astype(f32)
        pair = jnp.concatenate([a, b], axis=0).astype(bf16)
        out = nt(pair, leaf_basis[2 * c : 2 * c + 2].reshape(128, 256))
        joined.append(jnp.where(low, out[:8], out[8:]))

    skel = skeleton[...]
    xy = pltpu.roll(skel[:, :128], 64, 1)
    zz = jnp.concatenate([skel[:, 128:], skel[:, 128:]], axis=1)
    row = lax.broadcasted_iota(jnp.int32, (8, 128), 0)

    def skeleton_tile(m):
        x = xy[m : m + 1]
        y = skel[m : m + 1, :128]
        z = zz[m : m + 1]
        return jnp.where(row == 0, x, jnp.where(row == 1, y, jnp.where(row == 2, z, 0.0)))

    first = 0
    for level in range(1, 6):
        n = LEAVES >> level
        following = []
        for c in range(n // 2):
            high, lo = split(jnp.concatenate([joined[2 * c], joined[2 * c + 1]], axis=0))
            m = first + 2 * c
            out = nt(jnp.concatenate([high, lo], axis=0), transfer[m : m + 2].reshape(128, 128))
            out = out[:16] + out[16:]
            pair = jnp.where(low, out[:8], out[8:])
            following.append(pair)
            table[m] = jnp.where(low, pair, skeleton_tile(m))
            table[m + 1] = jnp.where(low, pltpu.roll(pair, 64, 1), skeleton_tile(m + 1))
        joined = following
        first += n
    high, lo = split(joined[0])
    stacked = jnp.concatenate([high.astype(f32), lo.astype(f32)], axis=0).astype(bf16)
    out = nt(stacked, transfer[62])
    out = out[:8] + out[8:]
    tile = jnp.where(low, jnp.concatenate([out, out], axis=1), skeleton_tile(62))
    table[62] = tile
    table[63] = jnp.zeros_like(tile)
    root[...] = tile

    for source, base in ((left, 0), (right, 32)):
        for t in range(32):
            rows = source[0:16, t * 256 : t * 256 + 256].astype(f32).T.astype(bf16)
            targets[base + t] = nn(rows, select[...]).astype(bf16)


def up(left, right, vectors, leaf_basis, near_list, transfer, skeleton):
    select = jnp.asarray(selection(), bf16)
    return pl.pallas_call(
        up_kernel,
        out_shape=(
            jax.ShapeDtypeStruct((64, 8, 128), f32),
            jax.ShapeDtypeStruct((8, 128), f32),
            jax.ShapeDtypeStruct((64, 256, 48), bf16),
            jax.ShapeDtypeStruct((LIST,), jnp.int32),
            jax.ShapeDtypeStruct((1,), jnp.int32),
        ),
        in_specs=[VM, VM, VM, VM, SM, VM, VM, VM],
        out_specs=(VM, VM, VM, SM, SM),
        compiler_params=params(32),
        name="up",
    )(left, right, vectors, leaf_basis, near_list, transfer, skeleton, select)


def near_kernel(piece, tiles, count, targets, w0, w1, w2, w3, order, start_field, field, token, window):
    window[:, 0:8192] = w0[...]
    window[:, 8192:16384] = w1[...]
    window[:, 16384:24576] = w2[...]
    window[:, 24576:32768] = w3[...]
    if piece == 0:
        field[...] = jnp.zeros_like(field)
    steps = (count[0] + UNROLL - 1) // UNROLL

    @pl.loop(steps * piece // PIECES, steps * (piece + 1) // PIECES)
    def _(g):
        results = []
        for u in range(UNROLL):
            code = tiles[g * UNROLL + u]
            t = code // 128
            at = pl.multiple_of((code % 128) * 256, 256)
            source = window[0:16, pl.ds(at, 256)]
            source = jnp.concatenate([source, source, source], axis=0)
            squares = nn(targets[jnp.minimum(t, LEAVES - 1)], source)
            squares = jnp.maximum(squares, 1e-30)
            tile = jnp.exp(-(squares * lax.rsqrt(squares))).astype(bf16)
            out = nt(window[16:32, pl.ds(at, 256)], tile)
            results.append((t, out[:8]))
        for t, out in results:
            field[t] += out

    token[...] = jnp.zeros_like(token)


def near(piece, tiles, count, targets, windows, order, start_field):
    aliases = {}
    if piece > 0:
        aliases = {8: 0}
    return pl.pallas_call(
        functools.partial(near_kernel, piece),
        out_shape=(
            jax.ShapeDtypeStruct((LEAVES + 1, 8, 256), f32),
            jax.ShapeDtypeStruct((8, 128), f32),
        ),
        in_specs=[SM, SM, VM, VM, VM, VM, VM, HB, VM if piece > 0 else HB],
        out_specs=(VM, VM),
        scratch_shapes=[pltpu.VMEM((32, 32768), bf16)],
        input_output_aliases=aliases,
        compiler_params=params(32),
        cost_estimate=pl.CostEstimate(flops=9_000_000_000, bytes_accessed=30_000_000, transcendentals=0),
        name="near%d" % piece,
    )(tiles, count, targets, *windows, order, start_field)


def pair_up(a, b, bit):
    low = low_lanes((8, 128))
    even = jnp.where(low, a, pltpu.roll(b, 64, 1))
    odd = jnp.where(low, b, pltpu.roll(a, 64, 1))
    return jnp.where(bit == 0, even, odd)


def lift(joined, matrix):
    high, lo = split(joined)
    stacked = jnp.concatenate([high.astype(f32), lo.astype(f32)], axis=0).astype(bf16)
    out = nt(stacked, matrix)
    out = out[:8] + out[8:]
    return jnp.concatenate([out, out], axis=1)


def lift_kernel(stage, dev, own, x1, x2, x3, ea, eb, ec, order, sibling, following):
    me = dev[0]
    bit0 = (me >> (2 * stage)) & 1
    bit1 = (me >> (2 * stage + 1)) & 1
    other = lift(pair_up(x2[...], x3[...], bit0), eb[0])
    sibling[...] = other
    if stage < 3:
        mine = lift(pair_up(own[...], x1[...], bit0), ea[0])
        following[...] = lift(pair_up(mine, other, bit1), ec[0])
    else:
        following[...] = other


def top_row(level, dev, flip=0):
    return 256 - (256 >> (level - 1)) + ((dev >> level) ^ flip)


def lift_round(stage, dev, own, x1, x2, x3, transfer_top, order):
    b = 2 * stage + 1
    full = pl.BlockSpec((8, 128), lambda i, d: (0, 0))
    shape = jax.ShapeDtypeStruct((8, 128), f32)
    return pl.pallas_call(
        functools.partial(lift_kernel, stage),
        out_shape=(shape, shape),
        grid_spec=pltpu.PrefetchScalarGridSpec(
            num_scalar_prefetch=1,
            grid=(1,),
            in_specs=[
                full,
                full,
                full,
                full,
                pl.BlockSpec((1, 64, 128), lambda i, d: (top_row(b, d[0]), 0, 0)),
                pl.BlockSpec((1, 64, 128), lambda i, d: (top_row(b, d[0], 1), 0, 0)),
                pl.BlockSpec((1, 64, 128), lambda i, d: (top_row(b + 1, d[0]), 0, 0)),
                HB,
            ],
            out_specs=(full, full),
        ),
        compiler_params=params(8),
        name="lift%d" % stage,
    )(dev, own, x1, x2, x3, transfer_top, transfer_top, transfer_top, order)


def down_kernel(
    dev,
    e1,
    e2,
    e3,
    e4,
    e5,
    e6,
    e7,
    e8,
    siblings,
    skeleton_top,
    far_list,
    table_left,
    table_own,
    table_right,
    transfer,
    leaf_basis,
    field,
    product,
    table,
    couple,
):
    me = dev[0]
    low = low_lanes((8, 128))
    row8 = lax.broadcasted_iota(jnp.int32, (8, 128), 0)
    table[0:64] = table_left[...]
    table[64:128] = table_own[...]
    table[128:192] = table_right[...]

    def columns(tile):
        turned = tile.T[64:128]
        return turned[:, 0:1], turned[:, 1:2], turned[:, 2:3]

    def coupling(cols, x, y, z):
        a = cols[0] - x
        b = cols[1] - y
        c = cols[2] - z
        return kernel_value(a * a + b * b + c * c)

    first = 0
    for level in range(1, 6):
        n = LEAVES >> level

        def pairs(c, carry, n=n, level=level, first=first):
            coefs = []
            values = []
            for h in range(2):
                j = 2 * c + h
                m = first + j
                coef_tiles = []
                skel_tiles = []
                for s in (0, 2):
                    parts = []
                    for k in (s, s + 1):
                        offset = far_list[m, k]
                        spot = j + offset
                        part = spot >> (6 - level)
                        at = (part + 1) * 64 + first + (spot & (n - 1))
                        parts.append((table[at], jnp.where(offset != 0, 1.0, 0.0).astype(f32)))
                    (ta, ua), (tb, ub) = parts
                    coef_tiles.append(jnp.where(low, ta * ua, pltpu.roll(tb, 64, 1) * ub))
                    skel_tiles.append(jnp.where(low, pltpu.roll(ta, 64, 1), tb))
                coef = jnp.concatenate(coef_tiles, axis=1)
                skel = jnp.concatenate(skel_tiles, axis=1)
                value = coupling(columns(table[64 + m]), skel[0:1], skel[1:2], skel[2:3])
                coefs.append(coef)
                values.append(value)
            c_high, c_low = split(jnp.concatenate(coefs, axis=0))
            v_high, v_low = split(jnp.concatenate(values, axis=0))
            out = nt(jnp.concatenate([c_high, c_low], axis=0), v_high)
            out = out[:16] + out[16:] + nt(c_high, v_low)
            couple[first // 2 + c] = jnp.where(low, out[:8], out[8:])
            return carry

        lax.fori_loop(0, n // 2, pairs, 0, unroll=min(4, n // 2))
        first += n

    def top_tile(index):
        line = skeleton_top[pl.ds(index, 1), :]
        x = jnp.concatenate([line[:, 0:64], line[:, 0:64]], axis=1)
        y = jnp.concatenate([line[:, 64:128], line[:, 64:128]], axis=1)
        z = jnp.concatenate([line[:, 128:192], line[:, 128:192]], axis=1)
        return jnp.where(row8 == 0, x, jnp.where(row8 == 1, y, jnp.where(row8 == 2, z, 0.0)))

    matrices = (e1, e2, e3, e4, e5, e6, e7, e8)
    added = []
    for b in range(8):
        other = siblings[b]
        if b == 0:
            own_tile = table[64 + 62]
            other_tile = other
        else:
            own_tile = top_tile(top_row(b, me))
            other_tile = top_tile(top_row(b, me, 1))
        value = coupling(
            columns(own_tile), other_tile[0:1, 64:128], other_tile[1:2, 64:128], other_tile[2:3, 64:128]
        )
        v_high, v_low = split(value)
        c_high, c_low = split(other[:, 0:64])
        stacked = jnp.concatenate([c_high.astype(f32), c_low.astype(f32)], axis=0).astype(bf16)
        out = nt(stacked, v_high)
        out2 = nt(stacked, v_low)
        added.append(out[:8] + out[8:] + out2[:8])
    current = added[7]
    for b in range(6, -1, -1):
        high, lo = split(current)
        stacked = jnp.concatenate([high.astype(f32), lo.astype(f32)], axis=0).astype(bf16)
        out = nn(stacked, matrices[b][0])
        out = out[:8] + out[8:]
        bit = (me >> b) & 1
        out = jnp.where(bit == 0, out, pltpu.roll(out, 64, 1))
        current = out[:, 0:64] + added[b]
    high, lo = split(current)
    stacked = jnp.concatenate([high.astype(f32), lo.astype(f32)], axis=0).astype(bf16)
    out = nn(stacked, transfer[62])
    fields = [out[:8] + out[8:] + couple[30]]

    def spread(tile):
        both = jnp.concatenate([jnp.where(low, tile, 0.0), jnp.where(low, 0.0, tile)], axis=0)
        high, lo = split(both)
        return jnp.concatenate([high, lo], axis=0)

    for level in range(4, -1, -1):
        above = 64 - (64 >> level)
        here = 64 - (64 >> (level - 1)) if level >= 1 else 0
        following = []
        for c, tile in enumerate(fields):
            m = above + 2 * c
            out = nn(spread(tile), transfer[m : m + 2].reshape(128, 128))
            out = out[:16] + out[16:]
            for h in range(2):
                piece = out[8 * h : 8 * h + 8]
                if level >= 1:
                    piece = piece + couple[here // 2 + 2 * c + h]
                following.append(piece)
        fields = following
    for c, tile in enumerate(fields):
        out = nn(spread(tile), leaf_basis[2 * c : 2 * c + 2].reshape(128, 256))
        out = out[:16] + out[16:]
        product[:, c * 512 : c * 512 + 256] = out[:8] + field[2 * c]
        product[:, c * 512 + 256 : c * 512 + 512] = out[8:] + field[2 * c + 1]


def down(
    dev, siblings, transfer_top, skeleton_top, far_list, tables, transfer, leaf_basis, field
):
    def whole(x):
        dims = x.ndim
        return pl.BlockSpec(x.shape, lambda i, d: (0,) * dims)

    matrix = [
        pl.BlockSpec((1, 64, 128), lambda i, d, b=b: (top_row(b, d[0]), 0, 0)) for b in range(1, 9)
    ]
    return pl.pallas_call(
        down_kernel,
        out_shape=jax.ShapeDtypeStruct((8, 16384), f32),
        grid_spec=pltpu.PrefetchScalarGridSpec(
            num_scalar_prefetch=1,
            grid=(1,),
            in_specs=matrix
            + [
                whole(siblings),
                whole(skeleton_top),
                SM,
                whole(tables[0]),
                whole(tables[1]),
                whole(tables[2]),
                whole(transfer),
                whole(leaf_basis),
                whole(field),
            ],
            out_specs=pl.BlockSpec((8, 16384), lambda i, d: (0, 0)),
            scratch_shapes=[pltpu.VMEM((192, 8, 128), f32), pltpu.VMEM((32, 8, 128), f32)],
        ),
        compiler_params=params(48),
        name="down",
    )(
        dev,
        *([transfer_top] * 8),
        siblings,
        skeleton_top,
        far_list,
        *tables,
        transfer,
        leaf_basis,
        field,
    )


def body(
    vectors, points, leaf_basis, near_list, far_list, transfer, skeleton, transfer_top, skeleton_top
):
    devices = lax.axis_size("dev")
    dev = lax.axis_index("dev").astype(jnp.int32).reshape(1)
    ends = devices - 1
    rightward = [(i, i + 1) for i in range(ends)]
    leftward = [(i + 1, i) for i in range(ends)]

    def exchange(x, mask):
        return lax.ppermute(x, "dev", [(i, i ^ mask) for i in range(devices)])

    left, right = prep(points, vectors)
    from_left = lax.ppermute(right, "dev", rightward)
    from_right = lax.ppermute(left, "dev", leftward)
    table, root, targets, tiles, count = up(
        left, right, vectors, leaf_basis, near_list, transfer, skeleton
    )
    table_left = lax.ppermute(table, "dev", rightward)
    table_right = lax.ppermute(table, "dev", leftward)
    windows = (from_left, left, right, from_right)
    own = root
    field = root
    siblings = []
    for stage in range(4):
        x1, x2, x3 = [exchange(own, k << (2 * stage)) for k in (1, 2, 3)]
        field, token = near(stage, tiles, count, targets, windows, own, field)
        sibling, own_next = lift_round(stage, dev, own, x1, x2, x3, transfer_top, token)
        siblings += [x1, sibling]
        own = own_next
    return down(
        dev,
        jnp.stack(siblings),
        transfer_top,
        skeleton_top,
        far_list,
        (table_left, table, table_right),
        transfer,
        leaf_basis,
        field,
    )


def solution(mesh):
    return jax.shard_map(
        body,
        mesh=mesh,
        in_specs=(
            P(None, "dev"),
            P(None, "dev"),
            P("dev", None, None),
            P("dev", None),
            P("dev", None),
            P("dev", None, None),
            P("dev", None),
            P(),
            P(),
        ),
        out_specs=P(None, "dev"),
        check_vma=False,
    )
```

```python
import functools

import jax
import jax.numpy as jnp
from jax import lax
from jax.experimental import pallas as pl
from jax.experimental.pallas import tpu as pltpu
from jax.sharding import PartitionSpec as P

f32 = jnp.float32
bf16 = jnp.bfloat16
LEAVES = 64
POINTS = 256
REACH = 32
RANK = 64
UNROLL = 24
PIECES = 7
MASKS = (1, 2, 6, 8, 24, 32, 64, 224)
LIST = 512 + UNROLL
VM = pl.BlockSpec(memory_space=pltpu.VMEM)
SM = pl.BlockSpec(memory_space=pltpu.SMEM)
HB = pl.BlockSpec(memory_space=pltpu.HBM)
DMA = pltpu.SemaphoreType.DMA


def params(mib):
    return pltpu.CompilerParams(vmem_limit_bytes=mib << 20)


def nt(a, b):
    return lax.dot_general(a, b, (((1,), (1,)), ((), ())), preferred_element_type=f32)


def nn(a, b):
    return jnp.dot(a, b, preferred_element_type=f32)


def split(x):
    high = x.astype(bf16)
    low = (x - high.astype(f32)).astype(bf16)
    return high, low


def low_lanes(shape):
    return lax.broadcasted_iota(jnp.int32, shape, 1) < RANK


def kernel_value(squares):
    return jnp.exp(-(squares * lax.rsqrt(jnp.maximum(squares, 1e-30))))


def prep_kernel(dev, points_hbm, vectors_hbm, send_a, send_b, targets, points, vectors, sems):
    copies = [
        pltpu.make_async_copy(points_hbm, points, sems.at[0]),
        pltpu.make_async_copy(vectors_hbm, vectors, sems.at[1]),
    ]
    for copy in copies:
        copy.start()
    for copy in copies:
        copy.wait()
    odd = (dev[0] & 1) == 1
    step = 512
    row = lax.broadcasted_iota(jnp.int32, (8, step), 0)
    for start in range(0, 16384, step):
        p = points[:, start : start + step]
        p = jnp.concatenate([p, jnp.zeros((5, step), f32)], axis=0)
        a1 = jnp.round(p * 64.0) * (1.0 / 64.0)
        rest = p - a1
        a2 = jnp.round(rest * 16384.0) * (1.0 / 16384.0)
        a3 = (rest - a2).astype(bf16).astype(f32)
        rest = a2 + a3
        big = jnp.sum(a1 * a1, axis=0, keepdims=True)
        small = jnp.sum((2.0 * a1 + rest) * rest, axis=0, keepdims=True)
        n1 = jnp.floor(big * 4.0) * 0.25
        big = big - n1
        n2 = jnp.floor(big * 1024.0) * (1.0 / 1024.0)
        value = (big - n2) + small
        n3 = value.astype(bf16).astype(f32)
        value = value - n3
        n4 = value.astype(bf16).astype(f32)
        n5 = value - n4
        upper = a1 + pltpu.roll(a2, 4, 0)
        upper = jnp.where((row == 3) | (row == 7), 1.0, upper)
        lower = jnp.where(row == 3, n1, a3)
        lower = jnp.where(row == 4, n2, lower)
        lower = jnp.where(row == 5, n3, lower)
        lower = jnp.where(row == 6, n4, lower)
        lower = jnp.where(row == 7, n5, lower)
        v = vectors[:, start : start + step].astype(f32)
        packed = jnp.concatenate([upper, lower, v, jnp.zeros_like(v)], axis=0).astype(bf16)
        copies = []
        for part, first, second, fill in ((a1, n1, n2, 1.0), (a2, n3, n4, 0.0), (a3, n5, 0.0, 0.0)):
            part = -2.0 * part
            top = part + pltpu.roll(part, 4, 0)
            top = jnp.where(row == 3, first, jnp.where(row == 7, second, top))
            copies += [top, jnp.where(row >= 3, fill, part)]
        targets[:, start : start + step] = jnp.concatenate(copies, axis=0).astype(bf16)
        at = start % 8192
        is_a = odd if start < 8192 else jnp.logical_not(odd)

        @pl.when(is_a)
        def _(packed=packed, at=at):
            send_a[:, at : at + step] = packed

        @pl.when(jnp.logical_not(is_a))
        def _(packed=packed, at=at):
            send_b[:, at : at + step] = packed


def prep(dev, points, vectors):
    shape = jax.ShapeDtypeStruct((32, 8192), bf16)
    return pl.pallas_call(
        prep_kernel,
        out_shape=(shape, shape, jax.ShapeDtypeStruct((48, 16384), bf16)),
        in_specs=[SM, HB, HB],
        out_specs=(VM, VM, VM),
        scratch_shapes=[pltpu.VMEM((3, 16384), f32), pltpu.VMEM((8, 16384), bf16), DMA((2,))],
        compiler_params=params(24),
        name="prep",
    )(dev, points, vectors)


def up_kernel(
    vectors_hbm,
    basis_hbm,
    near_list,
    transfer_hbm,
    skeleton_hbm,
    table,
    root,
    tiles,
    vectors,
    leaf_basis,
    transfer,
    skeleton,
    sems,
):
    copies = [
        pltpu.make_async_copy(vectors_hbm, vectors, sems.at[0]),
        pltpu.make_async_copy(basis_hbm, leaf_basis, sems.at[1]),
        pltpu.make_async_copy(transfer_hbm, transfer, sems.at[2]),
        pltpu.make_async_copy(skeleton_hbm, skeleton, sems.at[3]),
    ]
    for copy in copies:
        copy.start()

    def leaf_list(t, at):
        for s in range(8):
            offset = near_list[s, t]
            tiles[at] = t * 128 + t + REACH + offset
            if s == 0:
                at = at + 1
            else:
                at = at + jnp.where(offset != 0, 1, 0)
        return at

    total = lax.fori_loop(0, LEAVES, leaf_list, jnp.int32(0), unroll=4)
    for s in range(UNROLL):
        tiles[total + s] = LEAVES * 128 + REACH
    tiles[LIST] = total
    for copy in copies:
        copy.wait()

    low = low_lanes((8, 128))
    joined = []
    for c in range(LEAVES // 2):
        a = vectors[:, c * 512 : c * 512 + 256].astype(f32)
        b = vectors[:, c * 512 + 256 : c * 512 + 512].astype(f32)
        pair = jnp.concatenate([a, b], axis=0).astype(bf16)
        out = nt(pair, leaf_basis[2 * c : 2 * c + 2].reshape(128, 256))
        joined.append(jnp.where(low, out[:8], out[8:]))

    skel = skeleton[...]
    xy = pltpu.roll(skel[:, :128], 64, 1)
    zz = jnp.concatenate([skel[:, 128:], skel[:, 128:]], axis=1)
    row = lax.broadcasted_iota(jnp.int32, (8, 128), 0)

    def skeleton_tile(m):
        x = xy[m : m + 1]
        y = skel[m : m + 1, :128]
        z = zz[m : m + 1]
        return jnp.where(row == 0, x, jnp.where(row == 1, y, jnp.where(row == 2, z, 0.0)))

    first = 0
    for level in range(1, 6):
        n = LEAVES >> level
        following = []
        for c in range(n // 2):
            high, lo = split(jnp.concatenate([joined[2 * c], joined[2 * c + 1]], axis=0))
            m = first + 2 * c
            out = nt(jnp.concatenate([high, lo], axis=0), transfer[m : m + 2].reshape(128, 128))
            out = out[:16] + out[16:]
            pair = jnp.where(low, out[:8], out[8:])
            following.append(pair)
            table[m] = jnp.where(low, pair, skeleton_tile(m))
            table[m + 1] = jnp.where(low, pltpu.roll(pair, 64, 1), skeleton_tile(m + 1))
        joined = following
        first += n
    high, lo = split(joined[0])
    stacked = jnp.concatenate([high.astype(f32), lo.astype(f32)], axis=0).astype(bf16)
    out = nt(stacked, transfer[62])
    out = out[:8] + out[8:]
    tile = jnp.where(low, jnp.concatenate([out, out], axis=1), skeleton_tile(62))
    table[62] = tile
    table[63] = jnp.zeros_like(tile)
    root[...] = tile


def up(vectors, leaf_basis, near_list, transfer, skeleton):
    return pl.pallas_call(
        up_kernel,
        out_shape=(
            jax.ShapeDtypeStruct((64, 8, 128), f32),
            jax.ShapeDtypeStruct((8, 128), f32),
            jax.ShapeDtypeStruct((LIST + 1,), jnp.int32),
        ),
        in_specs=[HB, HB, SM, HB, HB],
        out_specs=(VM, VM, SM),
        scratch_shapes=[
            pltpu.VMEM(vectors.shape, bf16),
            pltpu.VMEM(leaf_basis.shape, bf16),
            pltpu.VMEM(transfer.shape, bf16),
            pltpu.VMEM(skeleton.shape, f32),
            DMA((4,)),
        ],
        compiler_params=params(24),
        name="up",
    )(vectors, leaf_basis, near_list, transfer, skeleton)


def near_kernel(piece, tiles, targets, *refs):
    if piece == 0:
        dev, send_a, send_b, from_a, from_b, field, token, window = refs
        odd = (dev[0] & 1) == 1

        @pl.when(odd)
        def _():
            for n, part in enumerate((from_a, send_a, send_b, from_b)):
                window[:, n * 8192 : n * 8192 + 8192] = part[...]

        @pl.when(jnp.logical_not(odd))
        def _():
            for n, part in enumerate((from_b, send_b, send_a, from_a)):
                window[:, n * 8192 : n * 8192 + 8192] = part[...]

        field[...] = jnp.zeros_like(field)
    else:
        window, order, start_field, field, token = refs
    steps = (tiles[LIST] + UNROLL - 1) // UNROLL

    @pl.loop(steps * piece // PIECES, steps * (piece + 1) // PIECES)
    def _(g):
        leaves = [tiles[g * UNROLL + u] // 128 for u in range(UNROLL)]
        before = [field[t] for t in leaves]
        sums = []
        for u, t in enumerate(leaves):
            at = pl.multiple_of((tiles[g * UNROLL + u] % 128) * 256, 256)
            mine = pl.multiple_of(jnp.minimum(t, LEAVES - 1) * 256, 256)
            source = window[0:16, pl.ds(at, 256)]
            source = jnp.concatenate([source, source, source], axis=0)
            squares = nn(targets[:, pl.ds(mine, 256)].T, source)
            squares = jnp.maximum(squares, 1e-30)
            tile = jnp.exp(-(squares * lax.rsqrt(squares))).astype(bf16)
            out = nt(window[16:32, pl.ds(at, 256)], tile)[:8]
            if u == 0:
                sums.append(before[0] + out)
            else:
                sums.append(jnp.where(t == leaves[u - 1], sums[u - 1], before[u]) + out)
        for t, total in zip(leaves, sums):
            field[t] = total

    token[...] = jnp.zeros_like(token)


def near(piece, tiles, targets, *rest):
    shapes = [
        jax.ShapeDtypeStruct((LEAVES + 1, 8, 256), f32),
        jax.ShapeDtypeStruct((8, 128), f32),
    ]
    if piece == 0:
        specs = [SM, VM, SM, VM, VM, VM, VM]
        shapes.append(jax.ShapeDtypeStruct((32, 32768), bf16))
        aliases = {}
    else:
        specs = [SM, VM, VM, VM, VM]
        aliases = {4: 0}
    return pl.pallas_call(
        functools.partial(near_kernel, piece),
        out_shape=tuple(shapes),
        in_specs=specs,
        out_specs=(VM,) * len(shapes),
        input_output_aliases=aliases,
        compiler_params=params(16),
        cost_estimate=pl.CostEstimate(flops=5_000_000_000, bytes_accessed=16_000_000, transcendentals=0),
        name="near%d" % piece,
    )(tiles, targets, *rest)


def pair_up(a, b, bit):
    low = low_lanes((8, 128))
    even = jnp.where(low, a, pltpu.roll(b, 64, 1))
    odd = jnp.where(low, b, pltpu.roll(a, 64, 1))
    return jnp.where(bit == 0, even, odd)


def lift(joined, matrix):
    high, lo = split(joined)
    stacked = jnp.concatenate([high.astype(f32), lo.astype(f32)], axis=0).astype(bf16)
    out = nt(stacked, matrix)
    out = out[:8] + out[8:]
    return jnp.concatenate([out, out], axis=1)


def lift_kernel(level, dev, own, sibling, matrix, order, *refs):
    following = refs[-1]
    if level == 2:
        table, table_copy, following = refs
        table_copy[...] = table[...]
    bit = (dev[0] >> (level - 1)) & 1
    other = sibling[0] if level == 1 else sibling[...]
    following[...] = lift(pair_up(own[...], other, bit), matrix[0])


def top_row(level, dev, flip=0):
    return 256 - (256 >> (level - 1)) + ((dev >> level) ^ flip)


def lift_round(level, dev, own, sibling, transfer_top, order, *table):
    full = pl.BlockSpec((8, 128), lambda i, d: (0, 0))
    shapes = [jax.ShapeDtypeStruct((8, 128), f32)]
    outs = [full]
    if table:
        shapes.insert(0, jax.ShapeDtypeStruct(table[0].shape, f32))
        outs.insert(0, VM)
    if level == 1:
        sibling_spec = pl.BlockSpec((1, 8, 128), lambda i, d: (62, 0, 0))
    else:
        sibling_spec = full
    return pl.pallas_call(
        functools.partial(lift_kernel, level),
        out_shape=tuple(shapes),
        grid_spec=pltpu.PrefetchScalarGridSpec(
            num_scalar_prefetch=1,
            grid=(1,),
            in_specs=[
                full,
                sibling_spec,
                pl.BlockSpec((1, 64, 128), lambda i, d: (top_row(level, d[0]), 0, 0)),
                VM,
            ]
            + [VM] * len(table),
            out_specs=tuple(outs),
        ),
        compiler_params=params(4),
        name="lift%d" % level,
    )(dev, own, sibling, transfer_top, order, *table)


def columns(tile):
    turned = tile.T[64:128]
    return turned[:, 0:1], turned[:, 1:2], turned[:, 2:3]


def coupling(cols, x, y, z):
    a = cols[0] - x
    b = cols[1] - y
    c = cols[2] - z
    return kernel_value(a * a + b * b + c * c)


def couple_kernel(
    dev, skeleton_top, far_list, table_own, table_a, table_b, order, couple, top_high, top_low, token, table
):
    me = dev[0]
    low = low_lanes((8, 128))
    row8 = lax.broadcasted_iota(jnp.int32, (8, 128), 0)
    table[64:128] = table_own[...]

    @pl.when((me & 1) == 1)
    def _():
        table[0:64] = table_a[...]
        table[128:192] = table_b[...]

    @pl.when((me & 1) == 0)
    def _():
        table[0:64] = table_b[...]
        table[128:192] = table_a[...]

    first = 0
    for level in range(1, 6):
        n = LEAVES >> level
        for c in range(n // 2):
            coefs = []
            values = []
            for h in range(2):
                j = 2 * c + h
                m = first + j
                coef_tiles = []
                skel_tiles = []
                for s in (0, 2):
                    parts = []
                    for k in (s, s + 1):
                        offset = far_list[k, m]
                        spot = j + offset
                        part = spot >> (6 - level)
                        at = (part + 1) * 64 + first + (spot & (n - 1))
                        parts.append((table[at], jnp.where(offset != 0, 1.0, 0.0).astype(f32)))
                    (ta, ua), (tb, ub) = parts
                    coef_tiles.append(jnp.where(low, ta * ua, pltpu.roll(tb, 64, 1) * ub))
                    skel_tiles.append(jnp.where(low, pltpu.roll(ta, 64, 1), tb))
                coef = jnp.concatenate(coef_tiles, axis=1)
                skel = jnp.concatenate(skel_tiles, axis=1)
                value = coupling(columns(table[64 + m]), skel[0:1], skel[1:2], skel[2:3])
                coefs.append(coef)
                values.append(value)
            c_high, c_low = split(jnp.concatenate(coefs, axis=0))
            v_high, v_low = split(jnp.concatenate(values, axis=0))
            out = nt(jnp.concatenate([c_high, c_low], axis=0), v_high)
            out = out[:16] + out[16:] + nt(c_high, v_low)
            couple[first // 2 + c] = jnp.where(low, out[:8], out[8:])
        first += n
    couple[31] = jnp.zeros((8, 128), f32)

    def top_tile(index):
        line = skeleton_top[pl.ds(index, 1), :]
        x = jnp.concatenate([line[:, 0:64], line[:, 0:64]], axis=1)
        y = jnp.concatenate([line[:, 64:128], line[:, 64:128]], axis=1)
        z = jnp.concatenate([line[:, 128:192], line[:, 128:192]], axis=1)
        return jnp.where(row8 == 0, x, jnp.where(row8 == 1, y, jnp.where(row8 == 2, z, 0.0)))

    for b in range(8):
        if b == 0:
            own_tile = table[64 + 62]
            other_tile = table_a[62]
        else:
            own_tile = top_tile(top_row(b, me))
            other_tile = top_tile(top_row(b, me, 1))
        value = coupling(
            columns(own_tile), other_tile[0:1, 64:128], other_tile[1:2, 64:128], other_tile[2:3, 64:128]
        )
        top_high[b], top_low[b] = split(value)
    token[...] = jnp.zeros_like(token)


def couple(dev, skeleton_top, far_list, tables, order):
    return pl.pallas_call(
        couple_kernel,
        out_shape=(
            jax.ShapeDtypeStruct((32, 8, 128), f32),
            jax.ShapeDtypeStruct((8, 64, 64), bf16),
            jax.ShapeDtypeStruct((8, 64, 64), bf16),
            jax.ShapeDtypeStruct((8, 128), f32),
        ),
        in_specs=[SM, VM, SM, VM, VM, VM, VM],
        out_specs=(VM,) * 4,
        scratch_shapes=[pltpu.VMEM((192, 8, 128), f32)],
        compiler_params=params(16),
        cost_estimate=pl.CostEstimate(flops=5_000_000_000, bytes_accessed=16_000_000, transcendentals=0),
        name="couple",
    )(dev, skeleton_top, far_list, *tables, order)


def twice(x):
    high, lo = split(x)
    return jnp.concatenate([high.astype(f32), lo.astype(f32)], axis=0).astype(bf16)


def down_kernel(
    dev,
    s1,
    s2,
    s3,
    s4,
    s5,
    s6,
    s7,
    top_hbm,
    table_a,
    couple,
    top_high,
    top_low,
    transfer_hbm,
    basis_hbm,
    field,
    order,
    product,
    top,
    transfer,
    leaf_basis,
    sems,
):
    me = dev[0]
    copies = [
        pltpu.make_async_copy(top_hbm.at[top_row(b, me)], top.at[b - 1], sems.at[b - 1])
        for b in range(1, 8)
    ]
    copies.append(pltpu.make_async_copy(transfer_hbm, transfer, sems.at[7]))
    basis_copy = pltpu.make_async_copy(basis_hbm, leaf_basis, sems.at[8])
    for copy in copies:
        copy.start()
    basis_copy.start()
    low = low_lanes((8, 128))

    siblings = (table_a[62], s1[...], s2[...], s3[...], s4[...], s5[...], s6[...], s7[...])
    added = []
    for b in range(8):
        stacked = twice(siblings[b][:, 0:64])
        out = nt(stacked, top_high[b])
        out2 = nt(stacked, top_low[b])
        added.append(out[:8] + out[8:] + out2[:8])
    for copy in copies:
        copy.wait()
    current = added[7]
    for b in range(6, -1, -1):
        out = nn(twice(current), top[b])
        out = out[:8] + out[8:]
        bit = (me >> b) & 1
        out = jnp.where(bit == 0, out, pltpu.roll(out, 64, 1))
        current = out[:, 0:64] + added[b]
    out = nn(twice(current), transfer[62])
    fields = [out[:8] + out[8:] + couple[30]]

    def spread(tile):
        both = jnp.concatenate([jnp.where(low, tile, 0.0), jnp.where(low, 0.0, tile)], axis=0)
        high, lo = split(both)
        return jnp.concatenate([high, lo], axis=0)

    for level in range(4, -1, -1):
        above = 64 - (64 >> level)
        here = 64 - (64 >> (level - 1)) if level >= 1 else 0
        following = []
        for c, tile in enumerate(fields):
            m = above + 2 * c
            out = nn(spread(tile), transfer[m : m + 2].reshape(128, 128))
            out = out[:16] + out[16:]
            for h in range(2):
                piece = out[8 * h : 8 * h + 8]
                if level >= 1:
                    piece = piece + couple[here // 2 + 2 * c + h]
                following.append(piece)
        fields = following
    basis_copy.wait()
    for c, tile in enumerate(fields):
        out = nn(spread(tile), leaf_basis[2 * c : 2 * c + 2].reshape(128, 256))
        out = out[:16] + out[16:]
        product[:, c * 512 : c * 512 + 256] = out[:8] + field[2 * c]
        product[:, c * 512 + 256 : c * 512 + 512] = out[8:] + field[2 * c + 1]


def down(dev, siblings, transfer_top, table_a, coupled, transfer, leaf_basis, field, order):
    return pl.pallas_call(
        down_kernel,
        out_shape=jax.ShapeDtypeStruct((8, 16384), f32),
        in_specs=[SM] + [VM] * 7 + [HB, VM, VM, VM, VM, HB, HB, VM, VM],
        out_specs=VM,
        scratch_shapes=[
            pltpu.VMEM((7, 64, 128), bf16),
            pltpu.VMEM(transfer.shape, bf16),
            pltpu.VMEM(leaf_basis.shape, bf16),
            DMA((9,)),
        ],
        compiler_params=params(16),
        name="down",
    )(dev, *siblings, transfer_top, table_a, *coupled, transfer, leaf_basis, field, order)


def body(
    vectors, points, leaf_basis, near_list, far_list, transfer, skeleton, transfer_top, skeleton_top
):
    devices = lax.axis_size("dev")
    dev = lax.axis_index("dev").astype(jnp.int32).reshape(1)

    def exchange(x, mask):
        return lax.ppermute(x, "dev", [(i, i ^ mask) for i in range(devices)])

    def exchange_outer(x):
        pairs = [(i, i + 1) for i in range(1, devices - 1, 2)]
        return lax.ppermute(x, "dev", pairs + [(j, i) for i, j in pairs])

    points, vectors, leaf_basis, transfer, skeleton = [
        pltpu.with_memory_space_constraint(x, pltpu.HBM)
        for x in (points, vectors, leaf_basis, transfer, skeleton)
    ]
    send_a, send_b, targets = prep(dev, points, vectors)
    from_a = exchange(send_a, 1)
    from_b = exchange_outer(send_b)
    table, own, tiles = up(vectors, leaf_basis, near_list.T, transfer, skeleton)
    table_a = exchange(table, 1)
    field, token, window = near(
        0, tiles, targets, dev, send_a, send_b, from_a, from_b
    )
    sibling = table_a
    siblings = []
    for level in range(1, 8):
        if level == 2:
            table_late, own = lift_round(level, dev, own, sibling, transfer_top, token, table)
            table_b = exchange_outer(table_late)
        else:
            (own,) = lift_round(level, dev, own, sibling, transfer_top, token)
        sibling = exchange(own, MASKS[level])
        siblings.append(sibling)
        if level < PIECES:
            field, token = near(level, tiles, targets, window, own, field)
    *coupled, token = couple(dev, skeleton_top, far_list.T, (table, table_a, table_b), own)
    return down(dev, siblings, transfer_top, table_a, coupled, transfer, leaf_basis, field, token)


def solution(mesh):
    return jax.shard_map(
        body,
        mesh=mesh,
        in_specs=(
            P(None, "dev"),
            P(None, "dev"),
            P("dev", None, None),
            P("dev", None),
            P("dev", None),
            P("dev", None, None),
            P("dev", None),
            P(),
            P(),
        ),
        out_specs=P(None, "dev"),
        check_vma=False,
    )
```

```python
import functools

import jax
import jax.numpy as jnp
from jax import lax
from jax.experimental import pallas as pl
from jax.experimental.pallas import tpu as pltpu
from jax.sharding import PartitionSpec as P

f32 = jnp.float32
bf16 = jnp.bfloat16
LEAVES = 64
POINTS = 256
REACH = 32
RANK = 64
UNROLL = 24
PIECES = 7
MASKS = (1, 2, 6, 8, 24, 32, 64, 224)
HALO = 512 + UNROLL
LIST = HALO + 448 + UNROLL
VM = pl.BlockSpec(memory_space=pltpu.VMEM)
SM = pl.BlockSpec(memory_space=pltpu.SMEM)
HB = pl.BlockSpec(memory_space=pltpu.HBM)
DMA = pltpu.SemaphoreType.DMA


def params(mib):
    return pltpu.CompilerParams(vmem_limit_bytes=mib << 20)


def nt(a, b):
    return lax.dot_general(a, b, (((1,), (1,)), ((), ())), preferred_element_type=f32)


def nn(a, b):
    return jnp.dot(a, b, preferred_element_type=f32)


def split(x):
    high = x.astype(bf16)
    low = (x - high.astype(f32)).astype(bf16)
    return high, low


def low_lanes(shape):
    return lax.broadcasted_iota(jnp.int32, shape, 1) < RANK


def kernel_value(squares):
    return jnp.exp(-(squares * lax.rsqrt(jnp.maximum(squares, 1e-30))))


def prep_kernel(
    dev,
    points_hbm,
    vectors_hbm,
    basis_hbm,
    transfer_hbm,
    send_a,
    send_b,
    targets,
    vectors,
    leaf_basis,
    transfer,
    points,
    sems,
):
    copies = [
        pltpu.make_async_copy(points_hbm, points, sems.at[0]),
        pltpu.make_async_copy(vectors_hbm, vectors, sems.at[1]),
    ]
    later = [
        pltpu.make_async_copy(basis_hbm, leaf_basis, sems.at[2]),
        pltpu.make_async_copy(transfer_hbm, transfer, sems.at[3]),
    ]
    for copy in copies + later:
        copy.start()
    for copy in copies:
        copy.wait()
    odd = (dev[0] & 1) == 1
    step = 512
    row = lax.broadcasted_iota(jnp.int32, (8, step), 0)
    for start in range(0, 16384, step):
        p = points[:, start : start + step]
        p = jnp.concatenate([p, jnp.zeros((5, step), f32)], axis=0)
        a1 = jnp.round(p * 64.0) * (1.0 / 64.0)
        rest = p - a1
        a2 = jnp.round(rest * 16384.0) * (1.0 / 16384.0)
        a3 = (rest - a2).astype(bf16).astype(f32)
        rest = a2 + a3
        big = jnp.sum(a1 * a1, axis=0, keepdims=True)
        small = jnp.sum((2.0 * a1 + rest) * rest, axis=0, keepdims=True)
        n1 = jnp.floor(big * 4.0) * 0.25
        big = big - n1
        n2 = jnp.floor(big * 1024.0) * (1.0 / 1024.0)
        value = (big - n2) + small
        n3 = value.astype(bf16).astype(f32)
        value = value - n3
        n4 = value.astype(bf16).astype(f32)
        n5 = value - n4
        upper = a1 + pltpu.roll(a2, 4, 0)
        upper = jnp.where((row == 3) | (row == 7), 1.0, upper)
        lower = jnp.where(row == 3, n1, a3)
        lower = jnp.where(row == 4, n2, lower)
        lower = jnp.where(row == 5, n3, lower)
        lower = jnp.where(row == 6, n4, lower)
        lower = jnp.where(row == 7, n5, lower)
        v = vectors[:, start : start + step].astype(f32)
        packed = jnp.concatenate([upper, lower, v, jnp.zeros_like(v)], axis=0).astype(bf16)
        copies = []
        for part, first, second, fill in ((a1, n1, n2, 1.0), (a2, n3, n4, 0.0), (a3, n5, 0.0, 0.0)):
            part = -2.0 * part
            top = part + pltpu.roll(part, 4, 0)
            top = jnp.where(row == 3, first, jnp.where(row == 7, second, top))
            copies += [top, jnp.where(row >= 3, fill, part)]
        targets[:, start : start + step] = jnp.concatenate(copies, axis=0).astype(bf16)
        at = start % 8192
        is_a = odd if start < 8192 else jnp.logical_not(odd)

        @pl.when(is_a)
        def _(packed=packed, at=at):
            send_a[:, at : at + step] = packed

        @pl.when(jnp.logical_not(is_a))
        def _(packed=packed, at=at):
            send_b[:, at : at + step] = packed

    for copy in later:
        copy.wait()


def prep(dev, points, vectors, leaf_basis, transfer):
    shape = jax.ShapeDtypeStruct((32, 8192), bf16)
    return pl.pallas_call(
        prep_kernel,
        out_shape=(
            shape,
            shape,
            jax.ShapeDtypeStruct((48, 16384), bf16),
            jax.ShapeDtypeStruct(vectors.shape, bf16),
            jax.ShapeDtypeStruct(leaf_basis.shape, bf16),
            jax.ShapeDtypeStruct(transfer.shape, bf16),
        ),
        in_specs=[SM, HB, HB, HB, HB],
        out_specs=(VM,) * 6,
        scratch_shapes=[pltpu.VMEM((3, 16384), f32), DMA((4,))],
        compiler_params=params(24),
        name="prep",
    )(dev, points, vectors, leaf_basis, transfer)


def up_kernel(near_list, vectors, leaf_basis, transfer, skeleton, table, root, tiles):
    def leaf_list(t, at):
        own, halo = at
        tiles[own] = t * 128 + t + REACH
        own = own + 1
        for s in range(1, 8):
            offset = near_list[s, t]
            partner = t + offset
            code = t * 128 + partner + REACH
            tiles[own] = code
            tiles[HALO + halo] = code
            used = jnp.where(offset != 0, 1, 0)
            inside = jnp.where((partner >= 0) & (partner < LEAVES), used, 0)
            own = own + inside
            halo = halo + (used - inside)
        return own, halo

    own, halo = lax.fori_loop(0, LEAVES, leaf_list, (jnp.int32(0), jnp.int32(0)), unroll=4)
    for s in range(UNROLL):
        tiles[own + s] = LEAVES * 128 + REACH
        tiles[HALO + halo + s] = LEAVES * 128 + REACH
    tiles[LIST] = own
    tiles[LIST + 1] = halo

    low = low_lanes((8, 128))
    joined = []
    for c in range(LEAVES // 2):
        a = vectors[:, c * 512 : c * 512 + 256].astype(f32)
        b = vectors[:, c * 512 + 256 : c * 512 + 512].astype(f32)
        pair = jnp.concatenate([a, b], axis=0).astype(bf16)
        out = nt(pair, leaf_basis[2 * c : 2 * c + 2].reshape(128, 256))
        joined.append(jnp.where(low, out[:8], out[8:]))

    skel = skeleton[...]
    xy = pltpu.roll(skel[:, :128], 64, 1)
    zz = jnp.concatenate([skel[:, 128:], skel[:, 128:]], axis=1)
    row = lax.broadcasted_iota(jnp.int32, (8, 128), 0)

    def skeleton_tile(m):
        x = xy[m : m + 1]
        y = skel[m : m + 1, :128]
        z = zz[m : m + 1]
        return jnp.where(row == 0, x, jnp.where(row == 1, y, jnp.where(row == 2, z, 0.0)))

    first = 0
    for level in range(1, 6):
        n = LEAVES >> level
        following = []
        for c in range(n // 2):
            high, lo = split(jnp.concatenate([joined[2 * c], joined[2 * c + 1]], axis=0))
            m = first + 2 * c
            out = nt(jnp.concatenate([high, lo], axis=0), transfer[m : m + 2].reshape(128, 128))
            out = out[:16] + out[16:]
            pair = jnp.where(low, out[:8], out[8:])
            following.append(pair)
            table[m] = jnp.where(low, pair, skeleton_tile(m))
            table[m + 1] = jnp.where(low, pltpu.roll(pair, 64, 1), skeleton_tile(m + 1))
        joined = following
        first += n
    high, lo = split(joined[0])
    stacked = jnp.concatenate([high.astype(f32), lo.astype(f32)], axis=0).astype(bf16)
    out = nt(stacked, transfer[62])
    out = out[:8] + out[8:]
    tile = jnp.where(low, jnp.concatenate([out, out], axis=1), skeleton_tile(62))
    table[62] = tile
    table[63] = jnp.zeros_like(tile)
    root[...] = tile


def up(near_list, vectors, leaf_basis, transfer, skeleton):
    return pl.pallas_call(
        up_kernel,
        out_shape=(
            jax.ShapeDtypeStruct((64, 8, 128), f32),
            jax.ShapeDtypeStruct((8, 128), f32),
            jax.ShapeDtypeStruct((LIST + 2,), jnp.int32),
        ),
        in_specs=[SM, VM, VM, VM, VM],
        out_specs=(VM, VM, SM),
        compiler_params=params(16),
        name="up",
    )(near_list, vectors, leaf_basis, transfer, skeleton)


def near_kernel(piece, tiles, targets, *refs):
    if piece == 0:
        dev, send_a, send_b, field, token, window = refs
        odd = (dev[0] & 1) == 1

        @pl.when(odd)
        def _():
            window[:, 8192:16384] = send_a[...]
            window[:, 16384:24576] = send_b[...]

        @pl.when(jnp.logical_not(odd))
        def _():
            window[:, 8192:16384] = send_b[...]
            window[:, 16384:24576] = send_a[...]

        field[...] = jnp.zeros_like(field)
    elif piece == 1:
        start_window, order, start_field, dev, from_a, from_b, field, token, window = refs
        odd = (dev[0] & 1) == 1

        @pl.when(odd)
        def _():
            window[:, 0:8192] = from_a[...]
            window[:, 24576:32768] = from_b[...]

        @pl.when(jnp.logical_not(odd))
        def _():
            window[:, 0:8192] = from_b[...]
            window[:, 24576:32768] = from_a[...]

    else:
        window, order, start_field, field, token = refs
    own_steps = (tiles[LIST] + UNROLL - 1) // UNROLL
    steps = own_steps + (tiles[LIST + 1] + UNROLL - 1) // UNROLL

    @pl.loop(steps * piece // PIECES, steps * (piece + 1) // PIECES)
    def _(g):
        first = jnp.where(g < own_steps, g * UNROLL, HALO + (g - own_steps) * UNROLL)
        leaves = [tiles[first + u] // 128 for u in range(UNROLL)]
        before = [field[t] for t in leaves]
        sums = []
        for u, t in enumerate(leaves):
            at = pl.multiple_of((tiles[first + u] % 128) * 256, 256)
            mine = pl.multiple_of(jnp.minimum(t, LEAVES - 1) * 256, 256)
            source = window[0:16, pl.ds(at, 256)]
            source = jnp.concatenate([source, source, source], axis=0)
            squares = nn(targets[:, pl.ds(mine, 256)].T, source)
            squares = jnp.maximum(squares, 1e-30)
            tile = jnp.exp(-(squares * lax.rsqrt(squares))).astype(bf16)
            out = nt(window[16:32, pl.ds(at, 256)], tile)[:8]
            if u == 0:
                sums.append(before[0] + out)
            else:
                sums.append(jnp.where(t == leaves[u - 1], sums[u - 1], before[u]) + out)
        for t, total in zip(leaves, sums):
            field[t] = total

    token[...] = jnp.zeros_like(token)


def near(piece, tiles, targets, *rest):
    shapes = [
        jax.ShapeDtypeStruct((LEAVES + 1, 8, 256), f32),
        jax.ShapeDtypeStruct((8, 128), f32),
    ]
    if piece < 2:
        shapes.append(jax.ShapeDtypeStruct((32, 32768), bf16))
    if piece == 0:
        specs = [SM, VM, SM, VM, VM]
        aliases = {}
    elif piece == 1:
        specs = [SM, VM, VM, VM, VM, SM, VM, VM]
        aliases = {2: 2, 4: 0}
    else:
        specs = [SM, VM, VM, VM, VM]
        aliases = {4: 0}
    return pl.pallas_call(
        functools.partial(near_kernel, piece),
        out_shape=tuple(shapes),
        in_specs=specs,
        out_specs=(VM,) * len(shapes),
        input_output_aliases=aliases,
        compiler_params=params(16),
        cost_estimate=pl.CostEstimate(flops=5_000_000_000, bytes_accessed=16_000_000, transcendentals=0),
        name="near%d" % piece,
    )(tiles, targets, *rest)


def pair_up(a, b, bit):
    low = low_lanes((8, 128))
    even = jnp.where(low, a, pltpu.roll(b, 64, 1))
    odd = jnp.where(low, b, pltpu.roll(a, 64, 1))
    return jnp.where(bit == 0, even, odd)


def lift(joined, matrix):
    high, lo = split(joined)
    stacked = jnp.concatenate([high.astype(f32), lo.astype(f32)], axis=0).astype(bf16)
    out = nt(stacked, matrix)
    out = out[:8] + out[8:]
    return jnp.concatenate([out, out], axis=1)


def lift_kernel(level, dev, own, sibling, matrix, order, *refs):
    following = refs[-1]
    if level == 2:
        table, table_copy, following = refs
        table_copy[...] = table[...]
    bit = (dev[0] >> (level - 1)) & 1
    other = sibling[0] if level == 1 else sibling[...]
    following[...] = lift(pair_up(own[...], other, bit), matrix[0])


def top_row(level, dev, flip=0):
    return 256 - (256 >> (level - 1)) + ((dev >> level) ^ flip)


def lift_round(level, dev, own, sibling, transfer_top, order, *table):
    full = pl.BlockSpec((8, 128), lambda i, d: (0, 0))
    shapes = [jax.ShapeDtypeStruct((8, 128), f32)]
    outs = [full]
    if table:
        shapes.insert(0, jax.ShapeDtypeStruct(table[0].shape, f32))
        outs.insert(0, VM)
    if level == 1:
        sibling_spec = pl.BlockSpec((1, 8, 128), lambda i, d: (62, 0, 0))
    else:
        sibling_spec = full
    return pl.pallas_call(
        functools.partial(lift_kernel, level),
        out_shape=tuple(shapes),
        grid_spec=pltpu.PrefetchScalarGridSpec(
            num_scalar_prefetch=1,
            grid=(1,),
            in_specs=[
                full,
                sibling_spec,
                pl.BlockSpec((1, 64, 128), lambda i, d: (top_row(level, d[0]), 0, 0)),
                VM,
            ]
            + [VM] * len(table),
            out_specs=tuple(outs),
        ),
        compiler_params=params(4),
        name="lift%d" % level,
    )(dev, own, sibling, transfer_top, order, *table)


def columns(turned, m):
    at = 8 * (m % 16)
    return turned[:, at : at + 1], turned[:, at + 1 : at + 2], turned[:, at + 2 : at + 3]


def coupling(cols, x, y, z):
    a = cols[0] - x
    b = cols[1] - y
    c = cols[2] - z
    return kernel_value(a * a + b * b + c * c)


def couple_kernel(
    dev, skeleton_top, far_list, table_own, table_a, table_b, order, couple, top_high, top_low, token, table, tops
):
    me = dev[0]
    low = low_lanes((8, 128))
    row8 = lax.broadcasted_iota(jnp.int32, (8, 128), 0)
    table[64:128] = table_own[...]

    @pl.when((me & 1) == 1)
    def _():
        table[0:64] = table_a[...]
        table[128:192] = table_b[...]

    @pl.when((me & 1) == 0)
    def _():
        table[0:64] = table_b[...]
        table[128:192] = table_a[...]

    turned = [table_own[16 * g : 16 * g + 16].reshape(128, 128).T[64:128] for g in range(4)]

    first = 0
    for level in range(1, 6):
        n = LEAVES >> level
        for c in range(n // 2):
            coefs = []
            values = []
            for h in range(2):
                j = 2 * c + h
                m = first + j
                coef_tiles = []
                skel_tiles = []
                for s in (0, 2):
                    parts = []
                    for k in (s, s + 1):
                        offset = far_list[k, m]
                        spot = j + offset
                        part = spot >> (6 - level)
                        at = (part + 1) * 64 + first + (spot & (n - 1))
                        parts.append((table[at], jnp.where(offset != 0, 1.0, 0.0).astype(f32)))
                    (ta, ua), (tb, ub) = parts
                    coef_tiles.append(jnp.where(low, ta * ua, pltpu.roll(tb, 64, 1) * ub))
                    skel_tiles.append(jnp.where(low, pltpu.roll(ta, 64, 1), tb))
                coef = jnp.concatenate(coef_tiles, axis=1)
                skel = jnp.concatenate(skel_tiles, axis=1)
                value = coupling(columns(turned[m // 16], m), skel[0:1], skel[1:2], skel[2:3])
                coefs.append(coef)
                values.append(value)
            c_high, c_low = split(jnp.concatenate(coefs, axis=0))
            v_high, v_low = split(jnp.concatenate(values, axis=0))
            out = nt(jnp.concatenate([c_high, c_low], axis=0), v_high)
            out = out[:16] + out[16:] + nt(c_high, v_low)
            couple[first // 2 + c] = jnp.where(low, out[:8], out[8:])
        first += n
    couple[31] = jnp.zeros((8, 128), f32)

    tops[0:128] = skeleton_top[:, 0:128].T
    tops[126:254] = skeleton_top[:, 126:254].T

    def top_tile(index):
        line = tops[pl.ds(index, 1), :]
        x = jnp.concatenate([line[:, 0:64], line[:, 0:64]], axis=1)
        y = jnp.concatenate([line[:, 64:128], line[:, 64:128]], axis=1)
        z = jnp.concatenate([line[:, 128:192], line[:, 128:192]], axis=1)
        return jnp.where(row8 == 0, x, jnp.where(row8 == 1, y, jnp.where(row8 == 2, z, 0.0)))

    own_tiles = [table_own[62]] + [top_tile(top_row(b, me)) for b in range(1, 8)]
    other_tiles = [table_a[62]] + [top_tile(top_row(b, me, 1)) for b in range(1, 8)]
    turned = jnp.concatenate(own_tiles + own_tiles, axis=0).T[64:128]
    for b, other in enumerate(other_tiles):
        value = coupling(columns(turned, b), other[0:1, 64:128], other[1:2, 64:128], other[2:3, 64:128])
        top_high[b], top_low[b] = split(value)
    token[...] = jnp.zeros_like(token)


def couple(dev, skeleton_top, far_list, tables, order):
    return pl.pallas_call(
        couple_kernel,
        out_shape=(
            jax.ShapeDtypeStruct((32, 8, 128), f32),
            jax.ShapeDtypeStruct((8, 64, 64), bf16),
            jax.ShapeDtypeStruct((8, 64, 64), bf16),
            jax.ShapeDtypeStruct((8, 128), f32),
        ),
        in_specs=[SM, VM, SM, VM, VM, VM, VM],
        out_specs=(VM,) * 4,
        scratch_shapes=[pltpu.VMEM((192, 8, 128), f32), pltpu.VMEM((254, 192), f32)],
        compiler_params=params(16),
        cost_estimate=pl.CostEstimate(flops=5_000_000_000, bytes_accessed=16_000_000, transcendentals=0),
        name="couple",
    )(dev, skeleton_top, far_list, *tables, order)


def twice(x):
    high, lo = split(x)
    return jnp.concatenate([high.astype(f32), lo.astype(f32)], axis=0).astype(bf16)


def down_kernel(
    dev,
    s1,
    s2,
    s3,
    s4,
    s5,
    s6,
    s7,
    top_hbm,
    table_a,
    couple,
    top_high,
    top_low,
    transfer,
    leaf_basis,
    field,
    order,
    product,
    top,
    sems,
):
    me = dev[0]
    copies = [
        pltpu.make_async_copy(top_hbm.at[top_row(b, me)], top.at[b - 1], sems.at[b - 1])
        for b in range(1, 8)
    ]
    for copy in copies:
        copy.start()
    low = low_lanes((8, 128))

    siblings = (table_a[62], s1[...], s2[...], s3[...], s4[...], s5[...], s6[...], s7[...])
    added = []
    for b in range(8):
        stacked = twice(siblings[b][:, 0:64])
        out = nt(stacked, top_high[b])
        out2 = nt(stacked, top_low[b])
        added.append(out[:8] + out[8:] + out2[:8])
    for copy in copies:
        copy.wait()
    current = added[7]
    for b in range(6, -1, -1):
        out = nn(twice(current), top[b])
        out = out[:8] + out[8:]
        bit = (me >> b) & 1
        out = jnp.where(bit == 0, out, pltpu.roll(out, 64, 1))
        current = out[:, 0:64] + added[b]
    out = nn(twice(current), transfer[62])
    fields = [out[:8] + out[8:] + couple[30]]

    def spread(tile):
        both = jnp.concatenate([jnp.where(low, tile, 0.0), jnp.where(low, 0.0, tile)], axis=0)
        high, lo = split(both)
        return jnp.concatenate([high, lo], axis=0)

    for level in range(4, -1, -1):
        above = 64 - (64 >> level)
        here = 64 - (64 >> (level - 1)) if level >= 1 else 0
        following = []
        for c, tile in enumerate(fields):
            m = above + 2 * c
            out = nn(spread(tile), transfer[m : m + 2].reshape(128, 128))
            out = out[:16] + out[16:]
            for h in range(2):
                piece = out[8 * h : 8 * h + 8]
                if level >= 1:
                    piece = piece + couple[here // 2 + 2 * c + h]
                following.append(piece)
        fields = following
    for c, tile in enumerate(fields):
        out = nn(spread(tile), leaf_basis[2 * c : 2 * c + 2].reshape(128, 256))
        out = out[:16] + out[16:]
        product[:, c * 512 : c * 512 + 256] = out[:8] + field[2 * c]
        product[:, c * 512 + 256 : c * 512 + 512] = out[8:] + field[2 * c + 1]


def down(dev, siblings, transfer_top, table_a, coupled, transfer, leaf_basis, field, order):
    return pl.pallas_call(
        down_kernel,
        out_shape=jax.ShapeDtypeStruct((8, 16384), f32),
        in_specs=[SM] + [VM] * 7 + [HB, VM, VM, VM, VM, VM, VM, VM, VM],
        out_specs=VM,
        scratch_shapes=[
            pltpu.VMEM((7, 64, 128), bf16),
            DMA((7,)),
        ],
        compiler_params=params(16),
        name="down",
    )(dev, *siblings, transfer_top, table_a, *coupled, transfer, leaf_basis, field, order)


def body(
    vectors, points, leaf_basis, near_list, far_list, transfer, skeleton, transfer_top, skeleton_top
):
    devices = lax.axis_size("dev")
    dev = lax.axis_index("dev").astype(jnp.int32).reshape(1)

    def exchange(x, mask):
        return lax.ppermute(x, "dev", [(i, i ^ mask) for i in range(devices)])

    def exchange_outer(x):
        pairs = [(i, i + 1) for i in range(1, devices - 1, 2)]
        return lax.ppermute(x, "dev", pairs + [(j, i) for i, j in pairs])

    points, vectors, leaf_basis, transfer = [
        pltpu.with_memory_space_constraint(x, pltpu.HBM)
        for x in (points, vectors, leaf_basis, transfer)
    ]
    send_a, send_b, targets, vectors, leaf_basis, transfer = prep(
        dev, points, vectors, leaf_basis, transfer
    )
    from_a = exchange(send_a, 1)
    from_b = exchange_outer(send_b)
    table, own, tiles = up(near_list.T, vectors, leaf_basis, transfer, skeleton)
    table_a = exchange(table, 1)
    field, token, window = near(0, tiles, targets, dev, send_a, send_b)
    sibling = table_a
    siblings = []
    for level in range(1, 8):
        if level == 2:
            table_late, own = lift_round(level, dev, own, sibling, transfer_top, token, table)
            table_b = exchange_outer(table_late)
        else:
            (own,) = lift_round(level, dev, own, sibling, transfer_top, token)
        sibling = exchange(own, MASKS[level])
        siblings.append(sibling)
        if level == 1:
            field, token, window = near(
                level, tiles, targets, window, own, field, dev, from_a, from_b
            )
        elif level < PIECES:
            field, token = near(level, tiles, targets, window, own, field)
    *coupled, token = couple(dev, skeleton_top.T, far_list.T, (table, table_a, table_b), own)
    return down(dev, siblings, transfer_top, table_a, coupled, transfer, leaf_basis, field, token)


def solution(mesh):
    return jax.shard_map(
        body,
        mesh=mesh,
        in_specs=(
            P(None, "dev"),
            P(None, "dev"),
            P("dev", None, None),
            P("dev", None),
            P("dev", None),
            P("dev", None, None),
            P("dev", None),
            P(),
            P(),
        ),
        out_specs=P(None, "dev"),
        check_vma=False,
    )
```

```python
import functools

import jax
import jax.numpy as jnp
from jax import lax
from jax.experimental import pallas as pl
from jax.experimental.pallas import tpu as pltpu
from jax.sharding import PartitionSpec as P

f32 = jnp.float32
bf16 = jnp.bfloat16
LEAVES = 64
POINTS = 256
REACH = 32
RANK = 64
UNROLL = 24
PIECES = 7
MASKS = (1, 2, 6, 8, 24, 32, 64, 224)
HALO = 512 + UNROLL
LIST = HALO + 448 + UNROLL
VM = pl.BlockSpec(memory_space=pltpu.VMEM)
SM = pl.BlockSpec(memory_space=pltpu.SMEM)
HB = pl.BlockSpec(memory_space=pltpu.HBM)
DMA = pltpu.SemaphoreType.DMA


def params(mib):
    return pltpu.CompilerParams(vmem_limit_bytes=mib << 20)


def nt(a, b):
    return lax.dot_general(a, b, (((1,), (1,)), ((), ())), preferred_element_type=f32)


def nn(a, b):
    return jnp.dot(a, b, preferred_element_type=f32)


def split(x):
    high = x.astype(bf16)
    low = (x - high.astype(f32)).astype(bf16)
    return high, low


def low_lanes(shape):
    return lax.broadcasted_iota(jnp.int32, shape, 1) < RANK


def kernel_value(squares):
    return jnp.exp(-(squares * lax.rsqrt(jnp.maximum(squares, 1e-30))))


def prep_kernel(
    dev,
    points_hbm,
    vectors_hbm,
    basis_hbm,
    transfer_hbm,
    send_a,
    send_b,
    targets,
    vectors,
    leaf_basis,
    transfer,
    points,
    sems,
):
    copies = [
        pltpu.make_async_copy(points_hbm, points, sems.at[0]),
        pltpu.make_async_copy(vectors_hbm, vectors, sems.at[1]),
    ]
    later = [
        pltpu.make_async_copy(basis_hbm, leaf_basis, sems.at[2]),
        pltpu.make_async_copy(transfer_hbm, transfer, sems.at[3]),
    ]
    for copy in copies:
        copy.start()
    for copy in copies:
        copy.wait()
    for copy in later:
        copy.start()
    odd = (dev[0] & 1) == 1
    step = 512
    row = lax.broadcasted_iota(jnp.int32, (8, step), 0)
    for start in range(0, 16384, step):
        p = points[:, start : start + step]
        p = jnp.concatenate([p, jnp.zeros((5, step), f32)], axis=0)
        a1 = jnp.round(p * 64.0) * (1.0 / 64.0)
        rest = p - a1
        a2 = jnp.round(rest * 16384.0) * (1.0 / 16384.0)
        a3 = (rest - a2).astype(bf16).astype(f32)
        rest = a2 + a3
        big = jnp.sum(a1 * a1, axis=0, keepdims=True)
        small = jnp.sum((2.0 * a1 + rest) * rest, axis=0, keepdims=True)
        n1 = jnp.floor(big * 4.0) * 0.25
        big = big - n1
        n2 = jnp.floor(big * 1024.0) * (1.0 / 1024.0)
        value = (big - n2) + small
        n3 = value.astype(bf16).astype(f32)
        value = value - n3
        n4 = value.astype(bf16).astype(f32)
        n5 = value - n4
        upper = a1 + pltpu.roll(a2, 4, 0)
        upper = jnp.where((row == 3) | (row == 7), 1.0, upper)
        lower = jnp.where(row == 3, n1, a3)
        lower = jnp.where(row == 4, n2, lower)
        lower = jnp.where(row == 5, n3, lower)
        lower = jnp.where(row == 6, n4, lower)
        lower = jnp.where(row == 7, n5, lower)
        v = vectors[:, start : start + step].astype(f32)
        packed = jnp.concatenate([upper, lower, v, jnp.zeros_like(v)], axis=0).astype(bf16)
        copies = []
        for part, first, second, fill in ((a1, n1, n2, 1.0), (a2, n3, n4, 0.0), (a3, n5, 0.0, 0.0)):
            part = -2.0 * part
            top = part + pltpu.roll(part, 4, 0)
            top = jnp.where(row == 3, first, jnp.where(row == 7, second, top))
            copies += [top, jnp.where(row >= 3, fill, part)]
        targets[:, start : start + step] = jnp.concatenate(copies, axis=0).astype(bf16)
        at = start % 8192
        is_a = odd if start < 8192 else jnp.logical_not(odd)

        @pl.when(is_a)
        def _(packed=packed, at=at):
            send_a[:, at : at + step] = packed

        @pl.when(jnp.logical_not(is_a))
        def _(packed=packed, at=at):
            send_b[:, at : at + step] = packed

    for copy in later:
        copy.wait()


def prep(dev, points, vectors, leaf_basis, transfer):
    shape = jax.ShapeDtypeStruct((32, 8192), bf16)
    return pl.pallas_call(
        prep_kernel,
        out_shape=(
            shape,
            shape,
            jax.ShapeDtypeStruct((48, 16384), bf16),
            jax.ShapeDtypeStruct(vectors.shape, bf16),
            jax.ShapeDtypeStruct(leaf_basis.shape, bf16),
            jax.ShapeDtypeStruct(transfer.shape, bf16),
        ),
        in_specs=[SM, HB, HB, HB, HB],
        out_specs=(VM,) * 6,
        scratch_shapes=[pltpu.VMEM((3, 16384), f32), DMA((4,))],
        compiler_params=params(24),
        name="prep",
    )(dev, points, vectors, leaf_basis, transfer)


def up_kernel(near_list, vectors, leaf_basis, transfer, skeleton, table, root, tiles):
    def leaf_list(t, at):
        own, halo = at
        tiles[own] = t * 128 + t + REACH
        own = own + 1
        for s in range(1, 8):
            offset = near_list[s, t]
            partner = t + offset
            code = t * 128 + partner + REACH
            tiles[own] = code
            tiles[HALO + halo] = code
            outside = (partner >> 6) & 1
            own = own + (jnp.where(offset != 0, 1, 0) - outside)
            halo = halo + outside
        return own, halo

    own, halo = lax.fori_loop(0, LEAVES, leaf_list, (jnp.int32(0), jnp.int32(0)), unroll=4)
    for s in range(UNROLL):
        tiles[own + s] = LEAVES * 128 + REACH
        tiles[HALO + halo + s] = LEAVES * 128 + REACH
    tiles[LIST] = own
    tiles[LIST + 1] = halo

    low = low_lanes((8, 128))
    joined = []
    for c in range(LEAVES // 2):
        a = vectors[:, c * 512 : c * 512 + 256].astype(f32)
        b = vectors[:, c * 512 + 256 : c * 512 + 512].astype(f32)
        pair = jnp.concatenate([a, b], axis=0).astype(bf16)
        out = nt(pair, leaf_basis[2 * c : 2 * c + 2].reshape(128, 256))
        joined.append(jnp.where(low, out[:8], out[8:]))

    skel = skeleton[...]
    xy = pltpu.roll(skel[:, :128], 64, 1)
    zz = jnp.concatenate([skel[:, 128:], skel[:, 128:]], axis=1)
    row = lax.broadcasted_iota(jnp.int32, (8, 128), 0)

    def skeleton_tile(m):
        x = xy[m : m + 1]
        y = skel[m : m + 1, :128]
        z = zz[m : m + 1]
        return jnp.where(row == 0, x, jnp.where(row == 1, y, jnp.where(row == 2, z, 0.0)))

    first = 0
    for level in range(1, 6):
        n = LEAVES >> level
        following = []
        for c in range(n // 2):
            high, lo = split(jnp.concatenate([joined[2 * c], joined[2 * c + 1]], axis=0))
            m = first + 2 * c
            out = nt(jnp.concatenate([high, lo], axis=0), transfer[m : m + 2].reshape(128, 128))
            out = out[:16] + out[16:]
            pair = jnp.where(low, out[:8], out[8:])
            following.append(pair)
            table[m] = jnp.where(low, pair, skeleton_tile(m))
            table[m + 1] = jnp.where(low, pltpu.roll(pair, 64, 1), skeleton_tile(m + 1))
        joined = following
        first += n
    high, lo = split(joined[0])
    stacked = jnp.concatenate([high.astype(f32), lo.astype(f32)], axis=0).astype(bf16)
    out = nt(stacked, transfer[62])
    out = out[:8] + out[8:]
    tile = jnp.where(low, jnp.concatenate([out, out], axis=1), skeleton_tile(62))
    table[62] = tile
    table[63] = jnp.zeros_like(tile)
    root[...] = tile


def up(near_list, vectors, leaf_basis, transfer, skeleton):
    return pl.pallas_call(
        up_kernel,
        out_shape=(
            jax.ShapeDtypeStruct((64, 8, 128), f32),
            jax.ShapeDtypeStruct((8, 128), f32),
            jax.ShapeDtypeStruct((LIST + 2,), jnp.int32),
        ),
        in_specs=[SM, VM, VM, VM, VM],
        out_specs=(VM, VM, SM),
        compiler_params=params(16),
        name="up",
    )(near_list, vectors, leaf_basis, transfer, skeleton)


def near_kernel(piece, tiles, targets, *refs):
    if piece == 0:
        dev, send_a, send_b, field, token, window = refs
        odd = (dev[0] & 1) == 1

        @pl.when(odd)
        def _():
            window[:, 8192:16384] = send_a[...]
            window[:, 16384:24576] = send_b[...]

        @pl.when(jnp.logical_not(odd))
        def _():
            window[:, 8192:16384] = send_b[...]
            window[:, 16384:24576] = send_a[...]

        field[...] = jnp.zeros_like(field)
    elif piece == 1:
        start_window, order, start_field, dev, from_a, from_b, field, token, window = refs
        odd = (dev[0] & 1) == 1

        @pl.when(odd)
        def _():
            window[:, 0:8192] = from_a[...]
            window[:, 24576:32768] = from_b[...]

        @pl.when(jnp.logical_not(odd))
        def _():
            window[:, 0:8192] = from_b[...]
            window[:, 24576:32768] = from_a[...]

    else:
        window, order, start_field, field, token = refs
    own_steps = (tiles[LIST] + UNROLL - 1) // UNROLL
    steps = own_steps + (tiles[LIST + 1] + UNROLL - 1) // UNROLL

    @pl.loop(steps * piece // PIECES, steps * (piece + 1) // PIECES)
    def _(g):
        first = jnp.where(g < own_steps, g * UNROLL, HALO + (g - own_steps) * UNROLL)
        leaves = [tiles[first + u] // 128 for u in range(UNROLL)]
        before = [field[t] for t in leaves]
        sums = []
        for u, t in enumerate(leaves):
            at = pl.multiple_of((tiles[first + u] % 128) * 256, 256)
            mine = pl.multiple_of(jnp.minimum(t, LEAVES - 1) * 256, 256)
            source = window[0:16, pl.ds(at, 256)]
            source = jnp.concatenate([source, source, source], axis=0)
            squares = nn(targets[:, pl.ds(mine, 256)].T, source)
            squares = jnp.maximum(squares, 1e-30)
            tile = jnp.exp(-(squares * lax.rsqrt(squares))).astype(bf16)
            out = nt(window[16:32, pl.ds(at, 256)], tile)[:8]
            if u == 0:
                sums.append(before[0] + out)
            else:
                sums.append(jnp.where(t == leaves[u - 1], sums[u - 1], before[u]) + out)
        for t, total in zip(leaves, sums):
            field[t] = total

    token[...] = jnp.zeros_like(token)


def near(piece, tiles, targets, *rest):
    shapes = [
        jax.ShapeDtypeStruct((LEAVES + 1, 8, 256), f32),
        jax.ShapeDtypeStruct((8, 128), f32),
    ]
    if piece < 2:
        shapes.append(jax.ShapeDtypeStruct((32, 32768), bf16))
    if piece == 0:
        specs = [SM, VM, SM, VM, VM]
        aliases = {}
    elif piece == 1:
        specs = [SM, VM, VM, VM, VM, SM, VM, VM]
        aliases = {2: 2, 4: 0}
    else:
        specs = [SM, VM, VM, VM, VM]
        aliases = {4: 0}
    return pl.pallas_call(
        functools.partial(near_kernel, piece),
        out_shape=tuple(shapes),
        in_specs=specs,
        out_specs=(VM,) * len(shapes),
        input_output_aliases=aliases,
        compiler_params=params(16),
        cost_estimate=pl.CostEstimate(flops=5_000_000_000, bytes_accessed=16_000_000, transcendentals=0),
        name="near%d" % piece,
    )(tiles, targets, *rest)


def pair_up(a, b, bit):
    low = low_lanes((8, 128))
    even = jnp.where(low, a, pltpu.roll(b, 64, 1))
    odd = jnp.where(low, b, pltpu.roll(a, 64, 1))
    return jnp.where(bit == 0, even, odd)


def lift(joined, matrix):
    high, lo = split(joined)
    stacked = jnp.concatenate([high.astype(f32), lo.astype(f32)], axis=0).astype(bf16)
    out = nt(stacked, matrix)
    out = out[:8] + out[8:]
    return jnp.concatenate([out, out], axis=1)


def lift_kernel(level, dev, own, sibling, matrix, order, *refs):
    following = refs[-1]
    if level == 2:
        table, table_copy, following = refs
        table_copy[...] = table[...]
    bit = (dev[0] >> (level - 1)) & 1
    other = sibling[0] if level == 1 else sibling[...]
    following[...] = lift(pair_up(own[...], other, bit), matrix[0])


def top_row(level, dev, flip=0):
    return 256 - (256 >> (level - 1)) + ((dev >> level) ^ flip)


def lift_round(level, dev, own, sibling, transfer_top, order, *table):
    full = pl.BlockSpec((8, 128), lambda i, d: (0, 0))
    shapes = [jax.ShapeDtypeStruct((8, 128), f32)]
    outs = [full]
    if table:
        shapes.insert(0, jax.ShapeDtypeStruct(table[0].shape, f32))
        outs.insert(0, VM)
    if level == 1:
        sibling_spec = pl.BlockSpec((1, 8, 128), lambda i, d: (62, 0, 0))
    else:
        sibling_spec = full
    return pl.pallas_call(
        functools.partial(lift_kernel, level),
        out_shape=tuple(shapes),
        grid_spec=pltpu.PrefetchScalarGridSpec(
            num_scalar_prefetch=1,
            grid=(1,),
            in_specs=[
                full,
                sibling_spec,
                pl.BlockSpec((1, 64, 128), lambda i, d: (top_row(level, d[0]), 0, 0)),
                VM,
            ]
            + [VM] * len(table),
            out_specs=tuple(outs),
        ),
        compiler_params=params(4),
        name="lift%d" % level,
    )(dev, own, sibling, transfer_top, order, *table)


def columns(turned, m):
    at = 8 * (m % 16)
    return turned[:, at : at + 1], turned[:, at + 1 : at + 2], turned[:, at + 2 : at + 3]


def coupling(cols, x, y, z):
    a = cols[0] - x
    b = cols[1] - y
    c = cols[2] - z
    return kernel_value(a * a + b * b + c * c)


def couple_kernel(
    dev, skeleton_top, far_list, table_own, table_a, table_b, order, couple, top_high, top_low, token, table, tops
):
    me = dev[0]
    low = low_lanes((8, 128))
    row8 = lax.broadcasted_iota(jnp.int32, (8, 128), 0)
    table[64:128] = table_own[...]

    @pl.when((me & 1) == 1)
    def _():
        table[0:64] = table_a[...]
        table[128:192] = table_b[...]

    @pl.when((me & 1) == 0)
    def _():
        table[0:64] = table_b[...]
        table[128:192] = table_a[...]

    turned = [table_own[16 * g : 16 * g + 16].reshape(128, 128).T[64:128] for g in range(4)]

    first = 0
    for level in range(1, 6):
        n = LEAVES >> level
        for c in range(n // 2):
            coefs = []
            values = []
            for h in range(2):
                j = 2 * c + h
                m = first + j
                coef_tiles = []
                skel_tiles = []
                for s in (0, 2):
                    parts = []
                    for k in (s, s + 1):
                        offset = far_list[k, m]
                        spot = j + offset
                        part = spot >> (6 - level)
                        at = (part + 1) * 64 + first + (spot & (n - 1))
                        parts.append((table[at], jnp.where(offset != 0, 1.0, 0.0).astype(f32)))
                    (ta, ua), (tb, ub) = parts
                    coef_tiles.append(jnp.where(low, ta * ua, pltpu.roll(tb, 64, 1) * ub))
                    skel_tiles.append(jnp.where(low, pltpu.roll(ta, 64, 1), tb))
                coef = jnp.concatenate(coef_tiles, axis=1)
                skel = jnp.concatenate(skel_tiles, axis=1)
                value = coupling(columns(turned[m // 16], m), skel[0:1], skel[1:2], skel[2:3])
                coefs.append(coef)
                values.append(value)
            c_high, c_low = split(jnp.concatenate(coefs, axis=0))
            v_high, v_low = split(jnp.concatenate(values, axis=0))
            out = nt(jnp.concatenate([c_high, c_low], axis=0), v_high)
            out = out[:16] + out[16:] + nt(c_high, v_low)
            couple[first // 2 + c] = jnp.where(low, out[:8], out[8:])
        first += n
    couple[31] = jnp.zeros((8, 128), f32)

    tops[0:128] = skeleton_top[:, 0:128].T
    tops[126:254] = skeleton_top[:, 126:254].T

    def top_tile(index):
        line = tops[pl.ds(index, 1), :]
        x = jnp.concatenate([line[:, 0:64], line[:, 0:64]], axis=1)
        y = jnp.concatenate([line[:, 64:128], line[:, 64:128]], axis=1)
        z = jnp.concatenate([line[:, 128:192], line[:, 128:192]], axis=1)
        return jnp.where(row8 == 0, x, jnp.where(row8 == 1, y, jnp.where(row8 == 2, z, 0.0)))

    own_tiles = [table_own[62]] + [top_tile(top_row(b, me)) for b in range(1, 8)]
    other_tiles = [table_a[62]] + [top_tile(top_row(b, me, 1)) for b in range(1, 8)]
    turned = jnp.concatenate(own_tiles + own_tiles, axis=0).T[64:128]
    for b, other in enumerate(other_tiles):
        value = coupling(columns(turned, b), other[0:1, 64:128], other[1:2, 64:128], other[2:3, 64:128])
        top_high[b], top_low[b] = split(value)
    token[...] = jnp.zeros_like(token)


def couple(dev, skeleton_top, far_list, tables, order):
    return pl.pallas_call(
        couple_kernel,
        out_shape=(
            jax.ShapeDtypeStruct((32, 8, 128), f32),
            jax.ShapeDtypeStruct((8, 64, 64), bf16),
            jax.ShapeDtypeStruct((8, 64, 64), bf16),
            jax.ShapeDtypeStruct((8, 128), f32),
        ),
        in_specs=[SM, VM, SM, VM, VM, VM, VM],
        out_specs=(VM,) * 4,
        scratch_shapes=[pltpu.VMEM((192, 8, 128), f32), pltpu.VMEM((254, 192), f32)],
        compiler_params=params(16),
        cost_estimate=pl.CostEstimate(flops=5_000_000_000, bytes_accessed=16_000_000, transcendentals=0),
        name="couple",
    )(dev, skeleton_top, far_list, *tables, order)


def twice(x):
    high, lo = split(x)
    return jnp.concatenate([high.astype(f32), lo.astype(f32)], axis=0).astype(bf16)


def down_kernel(
    dev,
    s1,
    s2,
    s3,
    s4,
    s5,
    s6,
    s7,
    top_hbm,
    table_a,
    couple,
    top_high,
    top_low,
    transfer,
    leaf_basis,
    field,
    order,
    product,
    top,
    sems,
):
    me = dev[0]
    copies = [
        pltpu.make_async_copy(top_hbm.at[top_row(b, me)], top.at[b - 1], sems.at[b - 1])
        for b in range(1, 8)
    ]
    for copy in copies:
        copy.start()
    low = low_lanes((8, 128))

    siblings = (table_a[62], s1[...], s2[...], s3[...], s4[...], s5[...], s6[...], s7[...])
    added = []
    for b in range(8):
        stacked = twice(siblings[b][:, 0:64])
        out = nt(stacked, top_high[b])
        out2 = nt(stacked, top_low[b])
        added.append(out[:8] + out[8:] + out2[:8])
    for copy in copies:
        copy.wait()
    current = added[7]
    for b in range(6, -1, -1):
        out = nn(twice(current), top[b])
        out = out[:8] + out[8:]
        bit = (me >> b) & 1
        out = jnp.where(bit == 0, out, pltpu.roll(out, 64, 1))
        current = out[:, 0:64] + added[b]
    out = nn(twice(current), transfer[62])
    fields = [out[:8] + out[8:] + couple[30]]

    def spread(tile):
        both = jnp.concatenate([jnp.where(low, tile, 0.0), jnp.where(low, 0.0, tile)], axis=0)
        high, lo = split(both)
        return jnp.concatenate([high, lo], axis=0)

    for level in range(4, -1, -1):
        above = 64 - (64 >> level)
        here = 64 - (64 >> (level - 1)) if level >= 1 else 0
        following = []
        for c, tile in enumerate(fields):
            m = above + 2 * c
            out = nn(spread(tile), transfer[m : m + 2].reshape(128, 128))
            out = out[:16] + out[16:]
            for h in range(2):
                piece = out[8 * h : 8 * h + 8]
                if level >= 1:
                    piece = piece + couple[here // 2 + 2 * c + h]
                following.append(piece)
        fields = following
    for c, tile in enumerate(fields):
        out = nn(spread(tile), leaf_basis[2 * c : 2 * c + 2].reshape(128, 256))
        out = out[:16] + out[16:]
        product[:, c * 512 : c * 512 + 256] = out[:8] + field[2 * c]
        product[:, c * 512 + 256 : c * 512 + 512] = out[8:] + field[2 * c + 1]


def down(dev, siblings, transfer_top, table_a, coupled, transfer, leaf_basis, field, order):
    return pl.pallas_call(
        down_kernel,
        out_shape=jax.ShapeDtypeStruct((8, 16384), f32),
        in_specs=[SM] + [VM] * 7 + [HB, VM, VM, VM, VM, VM, VM, VM, VM],
        out_specs=VM,
        scratch_shapes=[
            pltpu.VMEM((7, 64, 128), bf16),
            DMA((7,)),
        ],
        compiler_params=params(16),
        name="down",
    )(dev, *siblings, transfer_top, table_a, *coupled, transfer, leaf_basis, field, order)


def body(
    vectors, points, leaf_basis, near_list, far_list, transfer, skeleton, transfer_top, skeleton_top
):
    devices = lax.axis_size("dev")
    dev = lax.axis_index("dev").astype(jnp.int32).reshape(1)

    def exchange(x, mask):
        return lax.ppermute(x, "dev", [(i, i ^ mask) for i in range(devices)])

    def exchange_outer(x):
        pairs = [(i, i + 1) for i in range(1, devices - 1, 2)]
        return lax.ppermute(x, "dev", pairs + [(j, i) for i, j in pairs])

    points, vectors, leaf_basis, transfer = [
        pltpu.with_memory_space_constraint(x, pltpu.HBM)
        for x in (points, vectors, leaf_basis, transfer)
    ]
    send_a, send_b, targets, vectors, leaf_basis, transfer = prep(
        dev, points, vectors, leaf_basis, transfer
    )
    from_a = exchange(send_a, 1)
    from_b = exchange_outer(send_b)
    table, own, tiles = up(near_list.T, vectors, leaf_basis, transfer, skeleton)
    table_a = exchange(table, 1)
    field, token, window = near(0, tiles, targets, dev, send_a, send_b)
    sibling = table_a
    siblings = []
    for level in range(1, 8):
        if level == 2:
            table_late, own = lift_round(level, dev, own, sibling, transfer_top, token, table)
            table_b = exchange_outer(table_late)
        else:
            (own,) = lift_round(level, dev, own, sibling, transfer_top, token)
        sibling = exchange(own, MASKS[level])
        siblings.append(sibling)
        if level == 1:
            field, token, window = near(
                level, tiles, targets, window, own, field, dev, from_a, from_b
            )
        elif level < PIECES:
            field, token = near(level, tiles, targets, window, own, field)
    *coupled, token = couple(dev, skeleton_top.T, far_list.T, (table, table_a, table_b), own)
    return down(dev, siblings, transfer_top, table_a, coupled, transfer, leaf_basis, field, token)


def solution(mesh):
    return jax.shard_map(
        body,
        mesh=mesh,
        in_specs=(
            P(None, "dev"),
            P(None, "dev"),
            P("dev", None, None),
            P("dev", None),
            P("dev", None),
            P("dev", None, None),
            P("dev", None),
            P(),
            P(),
        ),
        out_specs=P(None, "dev"),
        check_vma=False,
    )
```
